128 devices in a mesh: rep: 8 (over z, x_hi), tp: 16 (over y, x_lo, core).
Axes of the slice: x: 4 (x_hi: 2, x_lo: 2; x = x_hi * 2 + x_lo), y: 4, z: 4, core: 2. Of those that a mesh axis runs over, the one named last changes fastest.
Arguments:
- tokens: bfloat16 [4096, 4096], P('rep', 'tp'), may hold values from -0.078125 to 0.078125
- noise: bfloat16 [8, 4096, 11008], P('rep', None, 'tp'), may hold values from -5 to 5
- cotangent: bfloat16 [4096, 11008], P('rep', 'tp'), may hold values from -30 to 30
- mean: float32 [4096, 11008], P('rep', 'tp'), may hold values from -5 to 5
- hess: float32 [4096, 11008], P('rep', 'tp'), may hold values from 0.5 to 2
- momentum: float32 [4096, 11008], P('rep', 'tp'), may hold values from -2 to 2
Outputs:
- new_mean: float32 [4096, 11008], P('rep', 'tp')
- new_hess: float32 [4096, 11008], P('rep', 'tp')
- new_momentum: float32 [4096, 11008], P('rep', 'tp')
- input_grad: bfloat16 [4096, 4096], P(('rep', 'tp'))
The draws below stay inside these ranges and needn't reach their ends.
All inputs are finite; a program needn't handle non-finite values.
Results may differ from the reference program's by a relative error of at most 0.007.
Values may be sent and summed in bfloat16 or wider, within the bound.
A program may use at most 128 MiB of HBM per device.

```python
import math
import jax
import jax.numpy as jnp
from jax import lax

D = 4096
FF = 11008
TOK_DEV = 512
TOKENS = 4096
N_REP = 8


def block_scale(rng, dims, shards, least, high):
    gain = 1.0
    for axis_at, parts in shards:
        heights = jax.random.uniform(jax.random.fold_in(jax.random.fold_in(rng, 6), axis_at), (parts,), jnp.float32, least / len(shards), high / len(shards))
        gain = gain * jnp.repeat(jnp.exp(heights), dims[axis_at] // parts).reshape((-1,) + (1,) * (len(dims) - 1 - axis_at))
    return gain


def bell_draw(key, shape, scale, bound, cuts=(), held_as=jnp.bfloat16):
    factor_of = block_scale(key, shape, cuts, -0.22, 0.18) if cuts else 1.0
    drawn = jax.random.normal(key, shape, jnp.float32) * scale * factor_of
    return jnp.minimum(jnp.maximum(drawn, -bound), bound).astype(held_as)


def setup_inputs(seed: int = 0) -> dict:
    arg_keys = jax.random.split(jax.random.key(seed), 7)
    tokens = bell_draw(arg_keys[0], (TOKENS, D), (D ** -0.5), 0.078125, ((0, 8), (1, 16)))
    noise = bell_draw(arg_keys[1], (N_REP, D, FF), 1.0, 5.0, ((0, 8), (2, 16)))
    cotangent = bell_draw(arg_keys[2], (TOKENS, FF), 5.0, 30.0, ((0, 8), (1, 16)))
    mean = bell_draw(arg_keys[3], (D, FF), 1.0, 5.0, ((0, 8), (1, 16)), jnp.float32)
    hess = jnp.clip(jnp.exp(math.log(2.0) - 1.3862944 * jax.random.uniform(arg_keys[4], (D, FF), jnp.float32) ** block_scale(arg_keys[4], (D, FF), ((0, 8), (1, 16)), -0.2, 0.2)), 0.5, 2.0)
    momentum = bell_draw(arg_keys[5], (D, FF), 0.3, 2.0, ((0, 8), (1, 16)), jnp.float32)
    return dict(tokens=tokens, noise=noise, cotangent=cotangent, mean=mean, hess=hess, momentum=momentum)


def reference(tokens, noise, cotangent, mean, hess, momentum):
    sigma = lax.rsqrt(4.0 * (hess + 0.001)).astype(jnp.bfloat16)
    mean_low = mean.astype(jnp.bfloat16)
    sigma_wide = sigma.astype(jnp.float32)
    token_blocks = tokens.reshape(N_REP, TOK_DEV, D)
    cot_blocks = cotangent.reshape(N_REP, TOK_DEV, FF)

    def replica(carry, index):
        grad_sum, hest_sum = carry
        feats = token_blocks[index]
        eps = noise[index].astype(jnp.float32)
        weight = (mean_low.astype(jnp.float32) + sigma_wide * eps).astype(jnp.bfloat16)
        pre = jnp.dot(feats, weight, preferred_element_type=jnp.float32)
        sig = jax.nn.sigmoid(pre)
        dpre = (cot_blocks[index].astype(jnp.float32) * sig * (1.0 + pre * (1.0 - sig))).astype(jnp.bfloat16)
        dinput = lax.dot_general(dpre, weight, (((1,), (1,)), ((), ())), preferred_element_type=jnp.float32)
        grad = lax.dot_general(feats, dpre, (((0,), (0,)), ((), ())), preferred_element_type=jnp.float32)
        hest = grad * eps / sigma_wide
        return ((grad_sum + grad, hest_sum + hest), dinput.astype(jnp.bfloat16))
    start = (jnp.zeros((D, FF), jnp.float32), jnp.zeros((D, FF), jnp.float32))
    (grad_sum, hest_sum), dinputs = lax.scan(replica, start, jnp.arange(N_REP, dtype=jnp.int32))
    grad_mean = grad_sum / N_REP
    hess_mean = hest_sum / N_REP
    new_momentum = 0.9 * momentum + 0.1 * grad_mean
    diff = hess - hess_mean
    new_hess = hess + 0.2 * (hess_mean - hess) + 0.5 * 0.04 * diff * diff / (hess + 0.001)
    new_mean = mean - 0.5 * (new_momentum + 0.001 * mean) / (new_hess + 0.001)
    return (new_mean, new_hess, new_momentum, dinputs.reshape(TOKENS, D))
```

```python
import functools

import jax
import jax.numpy as jnp
from jax import lax
from jax.experimental import pallas as pl
from jax.experimental.pallas import tpu as pltpu
from jax.sharding import PartitionSpec as P

MESH = pl.DeviceIdType.MESH
BF, F32 = jnp.bfloat16, jnp.float32

NZ, NY = 4, 4
UNITS, BLOCK, WIDE = 688, 512, 2048
HALF = 256
CHUNKS = ((0, 256), (256, 256), (512, 128), (640, 48))
EARLY = 2
PIECES = 2
PW = WIDE // PIECES
N_SEM = 128


def kernel(
    tok_in, noise_in, cot_in, mean_in, hess_in,
    sums_out, din_out,
    tok, tokt, n_own, n_par, ms, wt, cot, mean_v, hess_v,
    pre_own, p_send, p_recv, dp, dpt,
    g_send, g_recv, g_own, sums,
    c_send, c_recv, c_own, y_send, y_recv, y_own, l_send, l_recv, l_own, o_send, o_buf,
    ssem, rsem, lsem,
):
    rep, tp = lax.axis_index("rep"), lax.axis_index("tp")
    z, h = rep // 2, rep % 2
    y, l, c = tp // 4, (tp // 2) % 2, tp % 2

    def at(z=z, h=h, y=y, l=l, c=c):
        return (z * 2 + h, (y * 2 + l) * 2 + c)

    def zz(k):
        return lax.rem(z + k, NZ)

    def yy(k):
        return lax.rem(y + k, NY)

    partner, other_core, other_l = at(h=1 - h), at(c=1 - c), at(l=1 - l)

    def lanes(index, width, base=0):
        return pl.ds(pl.multiple_of(index * width + base, width if base == 0 else 256), width)

    count = [2]

    def remote(src, dst, device, slot=None, rslot=None):
        if slot is None:
            slot = count[0]
            count[0] += 1
        return pltpu.make_async_remote_copy(
            src_ref=src, dst_ref=dst, send_sem=ssem.at[slot], recv_sem=rsem.at[slot if rslot is None else rslot],
            device_id=device, device_id_type=MESH,
        )

    sent = []

    def send(*args, **kw):
        copy = remote(*args, **kw)
        copy.start()
        sent.append(copy)
        return copy

    peers = [other_l, partner, at(h=1 - h, l=1 - l), other_core]
    peers += [at(z=zz(k)) for k in (1, 2, 3)] + [at(y=yy(k)) for k in (1, 2, 3)]
    barrier = pltpu.get_barrier_semaphore()
    for peer in peers:
        pl.semaphore_signal(barrier, inc=1, device_id=peer, device_id_type=MESH)

    load_mean = pltpu.make_async_copy(mean_in, mean_v, lsem.at[0])
    load_hess = pltpu.make_async_copy(hess_in, hess_v, lsem.at[1])
    load_mean.start()
    load_hess.start()
    pl.semaphore_wait(barrier, len(peers))

    mine = lanes(y, 512, c * 256) if False else pl.ds(pl.multiple_of(y * 512 + c * 256, 256), 256)
    t_slot = tok.at[h, :, mine]
    t_near = remote(tok_in, t_slot, at(h=l, l=1 - l), slot=0, rslot=h)
    t_near.start()
    t_far = remote(tok_in, t_slot, partner, slot=1, rslot=h)
    t_self = pltpu.make_async_copy(tok_in, t_slot, rsem.at[h])
    stays = h == l

    @pl.when(stays)
    def _():
        t_self.start()

    @pl.when(jnp.logical_not(stays))
    def _():
        t_far.start()

    noise_copies = []

    def send_noise(k):
        first, rows = CHUNKS[k]
        noise_copies.append([
            send(
                noise_in.at[pl.ds(first, rows), pl.ds(pl.multiple_of((2 * b + 1 - h) * BLOCK, BLOCK), BLOCK)],
                n_par.at[pl.ds(first, rows), pl.ds(b * BLOCK, BLOCK)],
                partner,
            )
            for b in range(NZ)
        ])

    for k in range(EARLY):
        send_noise(k)

    load_own = []
    for b in range(NZ):
        load_own.append(
            pltpu.make_async_copy(
                noise_in.at[:, pl.ds(pl.multiple_of((2 * b + h) * BLOCK, BLOCK), BLOCK)],
                n_own.at[:, pl.ds(b * BLOCK, BLOCK)],
                lsem.at[3 + b],
            )
        )
        load_own[-1].start()
    load_cot = pltpu.make_async_copy(cot_in, cot, lsem.at[2])
    load_cot.start()

    load_mean.wait()
    load_hess.wait()
    own_z = pl.ds(pl.multiple_of(z * BLOCK, BLOCK), BLOCK)
    state_copies = []
    for first, rows in CHUNKS:

        @pl.loop(0, rows // 16)
        def _(i, first=first):
            r = pl.ds(pl.multiple_of(first + i * 16, 16), 16)
            ms[0, r, own_z] = mean_v[r, :].astype(BF)
            ms[1, r, own_z] = lax.rsqrt(4.0 * (hess_v[r, :] + 0.001)).astype(BF)

        part = ms.at[:, pl.ds(first, rows), own_z]
        state_copies.append([send(part, part, at(z=zz(k))) for k in (1, 3, 2)])

    for s in range(2):
        pltpu.make_async_copy(t_slot, tok.at[s, :, mine], rsem.at[s]).wait()
    block = tok.at[:, :, mine]
    y_copies = [send(block, block, at(y=yy(k))) for k in (1, 3, 2)]
    core_copies = [send(block, block, other_core)]
    for k, copy in zip((1, 3, 2), y_copies):
        copy.wait_recv()
        there = tok.at[:, :, pl.ds(pl.multiple_of(yy(4 - k) * 512 + c * 256, 256), 256)]
        core_copies.append(send(there, there, other_core))
    for copy in core_copies:
        copy.wait_recv()

    @pl.loop(0, 2 * WIDE // 256)
    def _(i):
        s, b = i // 8, i % 8
        f = pl.ds(pl.multiple_of(b * 256, 256), 256)
        tokt[s, f, :] = tok[s, :, f].T

    p_copies, d_copies, g_copies = {}, {}, {}
    sides = (h, 1 - h)

    def weights_and_pre(k):
        first, rows = CHUNKS[k]
        span = pl.ds(first, rows)
        for copy in state_copies[k] + noise_copies[k]:
            copy.wait_recv()

        @pl.loop(0, rows // 16)
        def _(i):
            r = pl.ds(pl.multiple_of(first + i * 16, 16), 16)
            for b in range(NZ):
                f = pl.ds(b * BLOCK, BLOCK)
                m, g = ms[0, r, f].astype(F32), ms[1, r, f].astype(F32)
                wt[0, r, f] = (m + g * n_own[r, f].astype(F32)).astype(BF)
                wt[1, r, f] = (m + g * n_par[r, f].astype(F32)).astype(BF)

        for half in range(2):
            t = pl.ds(half * HALF, HALF)
            p_send[span, t] = jnp.dot(
                wt[1, span, :], tokt[sides[1], :, t], preferred_element_type=F32
            ).astype(BF)
        p_copies[k] = send(p_send.at[span], p_recv.at[span], partner)
        for half in range(2):
            t = pl.ds(half * HALF, HALF)
            pre_own[span, t] = jnp.dot(wt[0, span, :], tokt[sides[0], :, t], preferred_element_type=F32)

    def dpre(k):
        first, rows = CHUNKS[k]
        span = pl.ds(first, rows)
        p_copies[k].wait_recv()

        @pl.loop(0, rows // 16)
        def _(i):
            r = pl.ds(pl.multiple_of(first + i * 16, 16), 16)
            pre = pre_own[r, :] + p_recv[r, :].astype(F32)
            sig = 1.0 / (1.0 + jnp.exp(-pre))
            dp[0, r, :] = (cot[r, :].astype(F32) * sig * (1.0 + pre * (1.0 - sig))).astype(BF)

        d_copies[k] = send(dp.at[0, span], dp.at[1, span], partner)
        turn(0, k)

    def turn(s, k):
        first, rows = CHUNKS[k]
        span = pl.ds(first, rows)
        for t in range(16):
            if t % 4 == 0:
                turned = dp[s, span, t * 32 : t * 32 + 128].T
            dpt[s, t % 2, pl.ds(t // 2 * 32, 32), span] = turned[t % 4 * 32 : t % 4 * 32 + 32, :]

    def grads(k):
        first, rows = CHUNKS[k]
        span = pl.ds(first, rows)
        g_copies[k] = []
        for step in (2, 1, 3, 0):
            for half in range(2):
                t = pl.ds(half * HALF, HALF)
                f = pl.ds(pl.multiple_of(zz(step) * BLOCK + half * HALF, HALF), HALF)
                one = jnp.dot(dp[0, span, :], tok[sides[0], :, f], preferred_element_type=F32)
                two = jnp.dot(dp[1, span, :], tok[sides[1], :, f], preferred_element_type=F32)
                hest = one * n_own[span, f].astype(F32) + two * n_par[span, f].astype(F32)
                if step:
                    g_send[step - 1, 0, span, t] = (one + two).astype(BF)
                    g_send[step - 1, 1, span, t] = hest.astype(BF)
                else:
                    g_own[0, span, t] = one + two
                    g_own[1, span, t] = hest
            if step:
                g_copies[k].append(
                    send(g_send.at[step - 1, :, span], g_recv.at[step - 1, :, span], at(z=zz(step)))
                )

    out_copies = []

    def finish_sums(k):
        first, rows = CHUNKS[k]
        span = pl.ds(first, rows)
        for copy in g_copies[k]:
            copy.wait_recv()

        @pl.loop(0, rows // 16)
        def _(i):
            r = pl.ds(pl.multiple_of(first + i * 16, 16), 16)
            total = [
                g_own[j, r, :]
                + (g_recv[0, j, r, :].astype(F32) + g_recv[1, j, r, :].astype(F32) + g_recv[2, j, r, :].astype(F32))
                for j in range(2)
            ]
            sums[0, r, :] = total[0]
            sums[1, r, :] = total[1] / ms[1, r, own_z].astype(F32)

        copy = pltpu.make_async_copy(sums.at[:, span], sums_out.at[:, span], lsem.at[7 + k])
        copy.start()
        out_copies.append(copy)

    c_copies, y_sends, l_copies, o_copies = {}, {}, {}, []

    def din_product(s, p):
        for which in (1 - c, c):
            for q in range(PW // HALF):
                f = pl.ds(p * PW + q * HALF, HALF)
                part = jnp.dot(dpt[s, which], wt[s, :, f], preferred_element_type=F32)
                if which is c:
                    c_own[s, :, f] = part
                else:
                    c_send[s, :, f] = part.astype(BF)
            if which is not c:
                f = pl.ds(p * PW, PW)
                c_copies[s, p] = send(c_send.at[s, :, f], c_recv.at[s, :, f], other_core)

    def din_y(s, p):
        c_copies[s, p].wait_recv()
        f = pl.ds(p * PW, PW)
        y_sends[s, p] = []
        for k in (2, 1, 3, 0):
            rows = pl.ds(pl.multiple_of(yy(k) * 64, 64), 64)
            part = c_own[s, rows, f] + c_recv[s, rows, f].astype(F32)
            if k:
                y_send[k - 1, s, :, f] = part.astype(BF)
                y_sends[s, p].append(
                    send(y_send.at[k - 1, s, :, f], y_recv.at[k - 1, s, :, f], at(y=yy(k)))
                )
            else:
                y_own[s, :, f] = part

    def din_l(s, p):
        for copy in y_sends[s, p]:
            copy.wait_recv()
        f = pl.ds(p * PW, PW)
        for which in (1 - l, l):
            rows = pl.ds(pl.multiple_of(which * 32, 32), 32)
            part = y_own[s, rows, f]
            for k in range(3):
                part = part + y_recv[k, s, rows, f].astype(F32)
            if which is l:
                l_own[s, :, f] = part
            else:
                l_send[s, :, f] = part.astype(BF)
                l_copies[s, p] = send(l_send.at[s, :, f], l_recv.at[s, :, f], other_l)

    def din_out_piece(s, p):
        l_copies[s, p].wait_recv()
        f = pl.ds(p * PW, PW)
        part = (l_own[s, :, f] + l_recv[s, :, f].astype(F32)).astype(BF)
        if s:
            o_send[:, f] = part
        for b in range(p * PW // BLOCK, (p + 1) * PW // BLOCK):
            there = pl.ds(pl.multiple_of((2 * b + h) * BLOCK, BLOCK), BLOCK)
            if s:
                o_copies.append(send(o_send.at[:, pl.ds(b * BLOCK, BLOCK)], o_buf.at[:, there], partner))
            else:
                o_buf[:, there] = part[:, (b * BLOCK - p * PW) : (b + 1) * BLOCK - p * PW]

    last = len(CHUNKS) - 1
    load_cot.wait()
    for copy in load_own:
        copy.wait()
    for k in range(last + 1):
        weights_and_pre(k)
        if k + EARLY <= last:
            send_noise(k + EARLY)
        if k:
            d_copies[k - 1].wait_recv()
            turn(1, k - 1)
            grads(k - 1)
        dpre(k)
    for p in range(PIECES):
        din_product(0, p)
    for p in range(PIECES):
        din_y(0, p)
    d_copies[last].wait_recv()
    turn(1, last)
    for p in range(PIECES):
        din_product(1, p)
    grads(last)
    for p in range(PIECES):
        din_y(1, p)
    for k in range(last):
        finish_sums(k)
    for p in range(PIECES):
        din_l(0, p)
    for p in range(PIECES):
        din_out_piece(0, p)
    finish_sums(last)
    for p in range(PIECES):
        din_l(1, p)
    for p in range(PIECES):
        din_out_piece(1, p)
    for copy in o_copies:
        copy.wait_recv()
    store = pltpu.make_async_copy(o_buf, din_out, lsem.at[2])
    store.start()
    store.wait()
    for copy in out_copies:
        copy.wait()
    t_near.wait_send()

    @pl.when(jnp.logical_not(stays))
    def _():
        t_far.wait_send()

    for copy in sent:
        copy.wait_send()


def communicate(tokens, noise, cotangent, mean, hess):
    vm = pltpu.VMEM
    units = (UNITS, BLOCK)
    scratch = [
        vm((2, BLOCK, WIDE), BF),
        vm((2, WIDE, BLOCK), BF),
        vm((UNITS, WIDE), BF),
        vm((UNITS, WIDE), BF),
        vm((2, UNITS, WIDE), BF),
        vm((2, UNITS, WIDE), BF),
        vm(units, BF),
        vm(units, F32),
        vm(units, F32),
        vm(units, F32),
        vm(units, BF),
        vm(units, BF),
        vm((2,) + units, BF),
        vm((2, 2, HALF, UNITS), BF),
        vm((3, 2) + units, BF),
        vm((3, 2) + units, BF),
        vm((2,) + units, F32),
        vm((2,) + units, F32),
        vm((2, HALF, WIDE), BF),
        vm((2, HALF, WIDE), BF),
        vm((2, HALF, WIDE), F32),
        vm((3, 2, 64, WIDE), BF),
        vm((3, 2, 64, WIDE), BF),
        vm((2, 64, WIDE), F32),
        vm((2, 32, WIDE), BF),
        vm((2, 32, WIDE), BF),
        vm((2, 32, WIDE), F32),
        vm((32, WIDE), BF),
        vm((32, 2 * WIDE), BF),
        pltpu.SemaphoreType.DMA((N_SEM,)),
        pltpu.SemaphoreType.DMA((N_SEM,)),
        pltpu.SemaphoreType.DMA((16,)),
    ]
    anywhere = pl.BlockSpec(memory_space=pl.ANY)
    return pl.pallas_call(
        kernel,
        out_shape=[
            jax.ShapeDtypeStruct((2,) + units, F32),
            jax.ShapeDtypeStruct((32, 2 * WIDE), BF),
        ],
        in_specs=[anywhere] * 5,
        out_specs=[anywhere] * 2,
        scratch_shapes=scratch,
        compiler_params=pltpu.CompilerParams(
            collective_id=1, has_side_effects=True, vmem_limit_bytes=62 << 20
        ),
        cost_estimate=pl.CostEstimate(flops=9 * 10**9, bytes_accessed=20 * 2**20, transcendentals=10**6),
    )(tokens, noise[0].T, cotangent.T, mean.T, hess.T)


def shards(tokens, noise, cotangent, mean, hess, momentum):
    n_rep = lax.axis_size("rep")
    sums, input_grad = communicate(tokens, noise, cotangent, mean, hess)
    grad_mean = sums[0].T / n_rep
    hess_mean = sums[1].T / n_rep
    new_momentum = 0.9 * momentum + 0.1 * grad_mean
    diff = hess - hess_mean
    new_hess = hess + 0.2 * (hess_mean - hess) + 0.5 * 0.04 * diff * diff / (hess + 0.001)
    new_mean = mean - 0.5 * (new_momentum + 0.001 * mean) / (new_hess + 0.001)
    return (new_mean, new_hess, new_momentum, input_grad)


def solution(mesh):
    in_specs = (
        P("rep", "tp"),
        P("rep", None, "tp"),
        P("rep", "tp"),
        P("rep", "tp"),
        P("rep", "tp"),
        P("rep", "tp"),
    )
    out_specs = (P("rep", "tp"), P("rep", "tp"), P("rep", "tp"), P(("rep", "tp"), None))
    return jax.shard_map(shards, mesh=mesh, in_specs=in_specs, out_specs=out_specs, check_vma=False)
```

```python
import jax
import jax.numpy as jnp
from jax import lax
from jax.experimental import pallas as pl
from jax.experimental.pallas import tpu as pltpu
from jax.sharding import PartitionSpec as P

MESH = pl.DeviceIdType.MESH
BF, F32 = jnp.bfloat16, jnp.float32

NZ, NY = 4, 4
UNITS, BLOCK, WIDE = 688, 512, 2048
HALF = 256
CHUNKS = ((0, 128), (128, 128), (256, 128), (384, 128), (512, 128), (640, 48))
LAST = len(CHUNKS) - 1
AHEAD_FIRST, AHEAD = 12, 10
PIECES = 2
PW = WIDE // PIECES
PH = PW // 2
N_SEM = 192


def kernel(
    tok_in, noise_in, cot_in, mean_in, hess_in, mom_in,
    mean_out, hess_out, mom_out, din_out,
    tok, tokt, n_own, n_par, ms, wt, cot, mean_v, hess_v, mom_v,
    pre_own, p_send, p_recv, dp, dpt,
    up_send, up_recv, dn_send, dn_recv, up2_send, up2_recv, dn2_send, dn2_recv, g_keep, g_own,
    c_send, c_recv, c_own, yu_send, yu_recv, yd_send, yd_recv, yu2_send, yu2_recv, yd2_send, yd2_recv,
    f_send, f_recv, f_own, o_buf,
    ssem, rsem, lsem,
):
    rep, tp = lax.axis_index("rep"), lax.axis_index("tp")
    z, h = rep // 2, rep % 2
    y, l, c = tp // 4, (tp // 2) % 2, tp % 2

    def at(z=z, h=h, y=y, l=l, c=c):
        return (z * 2 + h, (y * 2 + l) * 2 + c)

    def zz(k):
        return lax.rem(z + k, NZ)

    def yy(k):
        return lax.rem(y + k, NY)

    partner, other_core, other_l = at(h=1 - h), at(c=1 - c), at(l=1 - l)
    z_up, z_dn, y_up, y_dn = at(z=zz(1)), at(z=zz(3)), at(y=yy(1)), at(y=yy(3))
    count = [2]
    sent = []

    def remote(src, dst, device, slot, rslot):
        return pltpu.make_async_remote_copy(
            src_ref=src, dst_ref=dst, send_sem=ssem.at[slot], recv_sem=rsem.at[rslot],
            device_id=device, device_id_type=MESH,
        )

    def send(src, dst, device):
        slot = count[0]
        count[0] += 1
        copy = remote(src, dst, device, slot, slot)
        copy.start()
        sent.append(copy)
        return copy

    peers = [other_l, partner, at(h=1 - h, l=1 - l), other_core, z_up, z_dn, y_up, y_dn]
    barrier = pltpu.get_barrier_semaphore()
    for peer in peers:
        pl.semaphore_signal(barrier, inc=1, device_id=peer, device_id_type=MESH)

    loads = []

    def load(src, dst):
        copy = pltpu.make_async_copy(src, dst, lsem.at[len(loads)])
        copy.start()
        loads.append(copy)
        return copy

    load_mean, load_hess = load(mean_in, mean_v), load(hess_in, hess_v)
    pl.semaphore_wait(barrier, len(peers))

    def tok_slot(s, at_y):
        return tok.at[s, :, pl.ds(pl.multiple_of(at_y * 512 + c * 256, 256), 256)]

    t_near = remote(tok_in, tok_slot(h, y), at(h=l, l=1 - l), 0, h)
    t_near.start()
    t_far = remote(tok_in, tok_slot(h, y), partner, 1, h)
    t_self = pltpu.make_async_copy(tok_in, tok_slot(h, y), rsem.at[h])
    stays = h == l

    @pl.when(stays)
    def _():
        t_self.start()

    @pl.when(jnp.logical_not(stays))
    def _():
        t_far.start()

    n_copies = []

    def send_noise(upto):
        for n in range(len(n_copies), min(upto, NZ * len(CHUNKS))):
            (first, rows), b = CHUNKS[n // NZ], n % NZ
            n_copies.append(
                send(
                    noise_in.at[pl.ds(first, rows), pl.ds(pl.multiple_of((2 * b + 1 - h) * BLOCK, BLOCK), BLOCK)],
                    n_par.at[pl.ds(first, rows), pl.ds(b * BLOCK, BLOCK)],
                    partner,
                )
            )

    send_noise(AHEAD_FIRST)
    load_own = [
        load(
            noise_in.at[:, pl.ds(pl.multiple_of((2 * b + h) * BLOCK, BLOCK), BLOCK)],
            n_own.at[:, pl.ds(b * BLOCK, BLOCK)],
        )
        for b in range(NZ)
    ]
    load_cot, load_mom = load(cot_in, cot), load(mom_in, mom_v)

    def z_block(k):
        return pl.ds(pl.multiple_of(zz(k) * BLOCK, BLOCK), BLOCK)

    own_z = z_block(0)
    s_up, s_dn, s_up2, s_dn2 = {}, {}, {}, {}

    def state(k):
        first, rows = CHUNKS[k]

        @pl.loop(0, rows // 16)
        def _(i):
            r = pl.ds(pl.multiple_of(first + i * 16, 16), 16)
            ms[0, r, own_z] = mean_v[r, :].astype(BF)
            ms[1, r, own_z] = lax.rsqrt(4.0 * (hess_v[r, :] + 0.001)).astype(BF)

        part = ms.at[:, pl.ds(first, rows), own_z]
        s_up[k], s_dn[k] = send(part, part, z_up), send(part, part, z_dn)

    def state_on(k):
        span = pl.ds(*CHUNKS[k])
        s_up[k].wait_recv()
        part = ms.at[0, span, z_block(3)]
        s_up2[k] = send(part, part, z_up)
        s_dn[k].wait_recv()
        part = ms.at[1, span, z_block(1)]
        s_dn2[k] = send(part, part, z_dn)

    load_mean.wait()
    load_hess.wait()
    state(0)
    state(1)

    t_up, t_dn, core = [], [], []
    for s in (h, 1 - h):
        slot = tok_slot(s, y)
        pltpu.make_async_copy(slot, slot, rsem.at[s]).wait()
        t_up.append(send(slot, slot, y_up))
        t_dn.append(send(slot, slot, y_dn))
        core.append(send(slot, slot, other_core))

    def token_on(copy, slot, device=None):
        copy.wait_recv()
        core.append(send(slot, slot, other_core))
        return None if device is None else send(slot, slot, device)

    state_on(0)
    state(2)
    t_up2 = token_on(t_up[0], tok_slot(h, yy(3)), y_up)
    token_on(t_dn[0], tok_slot(h, yy(1)))
    state_on(1)
    state(3)
    t_dn2 = token_on(t_dn[1], tok_slot(1 - h, yy(1)), y_dn)
    token_on(t_up[1], tok_slot(1 - h, yy(3)))
    state_on(2)
    state(4)
    token_on(t_up2, tok_slot(h, yy(2)))
    token_on(t_dn2, tok_slot(1 - h, yy(2)))
    for copy in core:
        copy.wait_recv()

    @pl.loop(0, 2 * WIDE // 256)
    def _(i):
        s, b = i // 8, i % 8
        f = pl.ds(pl.multiple_of(b * 256, 256), 256)
        tokt[s, f, :] = tok[s, :, f].T

    p_copies, d_copies = {}, {}

    def weights_and_pre(k):
        first, rows = CHUNKS[k]
        span = pl.ds(first, rows)
        for copy in (s_up2[k], s_dn2[k], *n_copies[NZ * k : NZ * k + NZ]):
            copy.wait_recv()

        @pl.loop(0, rows // 16)
        def _(i):
            r = pl.ds(pl.multiple_of(first + i * 16, 16), 16)
            for b in range(NZ):
                f = pl.ds(b * BLOCK, BLOCK)
                m, g = ms[0, r, f].astype(F32), ms[1, r, f].astype(F32)
                wt[0, r, f] = (m + g * n_own[r, f].astype(F32)).astype(BF)
                wt[1, r, f] = (m + g * n_par[r, f].astype(F32)).astype(BF)

        for half in range(2):
            t = pl.ds(half * HALF, HALF)
            p_send[span, t] = jnp.dot(wt[1, span, :], tokt[1 - h, :, t], preferred_element_type=F32).astype(BF)
        p_copies[k] = send(p_send.at[span], p_recv.at[span], partner)
        for half in range(2):
            t = pl.ds(half * HALF, HALF)
            pre_own[span, t] = jnp.dot(wt[0, span, :], tokt[h, :, t], preferred_element_type=F32)

    def turn(s, k):
        span = pl.ds(*CHUNKS[k])
        for t in range(16):
            if t % 4 == 0:
                turned = dp[s, span, t * 32 : t * 32 + 128].T
            dpt[s, t % 2, pl.ds(t // 2 * 32, 32), span] = turned[t % 4 * 32 : t % 4 * 32 + 32, :]

    def dpre(k):
        first, rows = CHUNKS[k]
        span = pl.ds(first, rows)
        p_copies[k].wait_recv()

        @pl.loop(0, rows // 16)
        def _(i):
            r = pl.ds(pl.multiple_of(first + i * 16, 16), 16)
            pre = pre_own[r, :] + p_recv[r, :].astype(F32)
            sig = 1.0 / (1.0 + jnp.exp(-pre))
            dp[0, r, :] = (cot[r, :].astype(F32) * sig * (1.0 + pre * (1.0 - sig))).astype(BF)

        d_copies[k] = send(dp.at[0, span], dp.at[1, span], partner)

    g_up, g_dn, g_up2, g_dn2 = {}, {}, {}, {}

    def grads(k):
        span = pl.ds(*CHUNKS[k])
        for step in (2, 1, 3, 0):
            for half in range(2):
                t = pl.ds(half * HALF, HALF)
                f = pl.ds(pl.multiple_of(zz(step) * BLOCK + half * HALF, HALF), HALF)
                one = jnp.dot(dp[0, span, :], tok[h, :, f], preferred_element_type=F32)
                two = jnp.dot(dp[1, span, :], tok[1 - h, :, f], preferred_element_type=F32)
                grad, hest = one + two, one * n_own[span, f].astype(F32) + two * n_par[span, f].astype(F32)
                if step == 2:
                    up_send[0, span, t] = grad.astype(BF)
                    dn_send[0, span, t] = hest.astype(BF)
                elif step == 1:
                    g_keep[0, span, t] = grad
                    up_send[1, span, t] = hest.astype(BF)
                elif step == 3:
                    dn_send[1, span, t] = grad.astype(BF)
                    g_keep[1, span, t] = hest
                else:
                    g_own[0, span, t] = grad
                    g_own[1, span, t] = hest
            if step == 1:
                g_up[k] = send(up_send.at[:, span], up_recv.at[:, span], z_up)
            elif step == 3:
                g_dn[k] = send(dn_send.at[:, span], dn_recv.at[:, span], z_dn)

    def grads_on(k):
        first, rows = CHUNKS[k]
        span = pl.ds(first, rows)
        g_up[k].wait_recv()
        up2_send[span, :] = (g_keep[0, span, :] + up_recv[0, span, :].astype(F32)).astype(BF)
        g_up2[k] = send(up2_send.at[span], up2_recv.at[span], z_up)
        g_dn[k].wait_recv()
        dn2_send[span, :] = (g_keep[1, span, :] + dn_recv[0, span, :].astype(F32)).astype(BF)
        g_dn2[k] = send(dn2_send.at[span], dn2_recv.at[span], z_dn)

    stores = []

    def store(src, dst):
        copy = pltpu.make_async_copy(src, dst, lsem.at[len(loads) + len(stores)])
        copy.start()
        stores.append(copy)

    def update(k):
        first, rows = CHUNKS[k]
        span = pl.ds(first, rows)
        g_up2[k].wait_recv()
        g_dn2[k].wait_recv()

        @pl.loop(0, rows // 16)
        def _(i):
            r = pl.ds(pl.multiple_of(first + i * 16, 16), 16)
            mean, hess = mean_v[r, :], hess_v[r, :]
            grad_mean = (g_own[0, r, :] + dn_recv[1, r, :].astype(F32) + up2_recv[r, :].astype(F32)) / 8.0
            hest = (g_own[1, r, :] + up_recv[1, r, :].astype(F32) + dn2_recv[r, :].astype(F32)) / 8.0
            hess_mean = hest / ms[1, r, own_z].astype(F32)
            new_momentum = 0.9 * mom_v[r, :] + 0.1 * grad_mean
            diff = hess - hess_mean
            new_hess = hess + 0.2 * (hess_mean - hess) + 0.5 * 0.04 * diff * diff / (hess + 0.001)
            mom_v[r, :] = new_momentum
            hess_v[r, :] = new_hess
            mean_v[r, :] = mean - 0.5 * (new_momentum + 0.001 * mean) / (new_hess + 0.001)

        store(mean_v.at[span], mean_out.at[span])
        store(hess_v.at[span], hess_out.at[span])
        store(mom_v.at[span], mom_out.at[span])

    c_copies, y_up1, y_dn1, y_up2, y_dn2, f_copies = {}, {}, {}, {}, {}, {}

    def din_product(s, p, keep):
        f = pl.ds(p * PW, PW)
        for q in range(PW // HALF):
            g = pl.ds(p * PW + q * HALF, HALF)
            part = jnp.dot(dpt[s, c if keep else 1 - c], wt[s, :, g], preferred_element_type=F32)
            if keep:
                c_own[s, :, g] = part
            else:
                c_send[s, :, g] = part.astype(BF)
        if not keep:
            c_copies[s, p] = send(c_send.at[s, :, f], c_recv.at[s, :, f], other_core)

    def din_products(s):
        for keep in (False, True):
            for p in range(PIECES):
                din_product(s, p, keep)

    def din_sum(s, p, k, second):
        rows = pl.ds(pl.multiple_of(yy(k) * 64, 64), 64)
        g = pl.ds(p * PW + second * PH, PH)
        return c_own[s, rows, g] + c_recv[s, rows, g].astype(F32)

    def din_y(s, p):
        c_copies[s, p].wait_recv()
        yu_send[s, p, 0] = din_sum(s, p, 2, 0).astype(BF)
        yu_send[s, p, 1] = din_sum(s, p, 1, 1).astype(BF)
        y_up1[s, p] = send(yu_send.at[s, p], yu_recv.at[s, p], y_up)
        yd_send[s, p, 0] = din_sum(s, p, 2, 1).astype(BF)
        yd_send[s, p, 1] = din_sum(s, p, 3, 0).astype(BF)
        y_dn1[s, p] = send(yd_send.at[s, p], yd_recv.at[s, p], y_dn)

    def din_y_on(s, p):
        y_up1[s, p].wait_recv()
        yu2_send[s, p] = (din_sum(s, p, 1, 0) + yu_recv[s, p, 0].astype(F32)).astype(BF)
        y_up2[s, p] = send(yu2_send.at[s, p], yu2_recv.at[s, p], y_up)
        y_dn1[s, p].wait_recv()
        yd2_send[s, p] = (din_sum(s, p, 3, 1) + yd_recv[s, p, 0].astype(F32)).astype(BF)
        y_dn2[s, p] = send(yd2_send.at[s, p], yd2_recv.at[s, p], y_dn)

    def din_last(s, p):
        y_up2[s, p].wait_recv()
        y_dn2[s, p].wait_recv()
        f = pl.ds(p * PW, PW)
        f_copies[s, p] = []
        for near in (False, True):
            which = l if near else 1 - l
            mine = pl.ds(pl.multiple_of(y * 64 + which * 32, 32), 32)
            rows = pl.ds(pl.multiple_of(which * 32, 32), 32)
            for second in range(2):
                g = pl.ds(p * PW + second * PH, PH)
                part = c_own[s, mine, g] + c_recv[s, mine, g].astype(F32)
                if second:
                    part = part + yu_recv[s, p, 1, rows, :].astype(F32) + yd2_recv[s, p, rows, :].astype(F32)
                else:
                    part = part + yd_recv[s, p, 1, rows, :].astype(F32) + yu2_recv[s, p, rows, :].astype(F32)
                if near and not s:
                    f_own[:, g] = part
                else:
                    f_send[s + near, :, g] = part.astype(BF)
            if s or not near:
                there = partner if near else at(h=1 - h, l=1 - l) if s else other_l
                f_copies[s, p].append(send(f_send.at[s + near, :, f], f_recv.at[s + near, :, f], there))

    def din_end(s, p):
        for copy in f_copies[s, p]:
            copy.wait_recv()
        for b in range(p * PW // BLOCK, (p + 1) * PW // BLOCK):
            f = pl.ds(b * BLOCK, BLOCK)
            there = pl.ds(pl.multiple_of((2 * b + (1 - h if s else h)) * BLOCK, BLOCK), BLOCK)
            if s:
                part = f_recv[1, :, f].astype(F32) + f_recv[2, :, f].astype(F32)
            else:
                part = f_own[:, f] + f_recv[0, :, f].astype(F32)
            o_buf[:, there] = part.astype(BF)

    load_cot.wait()
    for copy in load_own:
        copy.wait()
    for k in range(LAST + 1):
        weights_and_pre(k)
        if k == 0:
            send_noise(NZ + AHEAD)
            state_on(3)
            state(5)
        if k == 1:
            state_on(4)
        if k >= 1:
            dpre(k - 1)
            send_noise(NZ * (k + 1) + AHEAD)
            turn(0, k - 1)
        if k == 2:
            state_on(5)
        if k >= 2:
            d_copies[k - 2].wait_recv()
            grads(k - 2)
            turn(1, k - 2)
        if k >= 3:
            grads_on(k - 3)
        if k == 3:
            load_mom.wait()
        if k >= 4:
            update(k - 4)
    dpre(LAST)
    turn(0, LAST)
    din_products(0)
    d_copies[LAST - 1].wait_recv()
    grads(LAST - 1)
    turn(1, LAST - 1)
    din_y(0, 0)
    din_y(0, 1)
    grads_on(LAST - 2)
    d_copies[LAST].wait_recv()
    turn(1, LAST)
    din_products(1)
    grads(LAST)
    din_y_on(0, 0)
    din_y(1, 0)
    din_y_on(0, 1)
    din_y(1, 1)
    update(LAST - 3)
    grads_on(LAST - 1)
    din_y_on(1, 0)
    din_last(0, 0)
    din_last(0, 1)
    grads_on(LAST)
    update(LAST - 2)
    din_y_on(1, 1)
    din_last(1, 0)
    din_end(0, 0)
    din_end(0, 1)
    update(LAST - 1)
    din_last(1, 1)
    update(LAST)
    din_end(1, 0)
    din_end(1, 1)
    store(o_buf, din_out)
    for copy in stores:
        copy.wait()
    t_near.wait_send()

    @pl.when(jnp.logical_not(stays))
    def _():
        t_far.wait_send()

    for copy in sent:
        copy.wait_send()


def shards(tokens, noise, cotangent, mean, hess, momentum):
    vm = pltpu.VMEM
    units = (UNITS, BLOCK)
    piece = (2, PIECES, 64, PH)
    scratch = [
        vm((2, BLOCK, WIDE), BF),
        vm((2, WIDE, BLOCK), BF),
        vm((UNITS, WIDE), BF),
        vm((UNITS, WIDE), BF),
        vm((2, UNITS, WIDE), BF),
        vm((2, UNITS, WIDE), BF),
        vm(units, BF),
        vm(units, F32),
        vm(units, F32),
        vm(units, F32),
        vm(units, F32),
        vm(units, BF),
        vm(units, BF),
        vm((2,) + units, BF),
        vm((2, 2, HALF, UNITS), BF),
        *[vm((2,) + units, BF)] * 4,
        *[vm(units, BF)] * 4,
        vm((2,) + units, F32),
        vm((2,) + units, F32),
        vm((2, HALF, WIDE), BF),
        vm((2, HALF, WIDE), BF),
        vm((2, HALF, WIDE), F32),
        *[vm((2, PIECES, 2, 64, PH), BF)] * 4,
        *[vm(piece, BF)] * 4,
        vm((3, 32, WIDE), BF),
        vm((3, 32, WIDE), BF),
        vm((32, WIDE), F32),
        vm((32, 2 * WIDE), BF),
        pltpu.SemaphoreType.DMA((N_SEM,)),
        pltpu.SemaphoreType.DMA((N_SEM,)),
        pltpu.SemaphoreType.DMA((32,)),
    ]
    anywhere = pl.BlockSpec(memory_space=pl.ANY)
    new_mean, new_hess, new_momentum, input_grad = pl.pallas_call(
        kernel,
        out_shape=[jax.ShapeDtypeStruct(units, F32)] * 3 + [jax.ShapeDtypeStruct((32, 2 * WIDE), BF)],
        in_specs=[anywhere] * 6,
        out_specs=[anywhere] * 4,
        scratch_shapes=scratch,
        compiler_params=pltpu.CompilerParams(
            collective_id=1, has_side_effects=True, vmem_limit_bytes=63 << 20
        ),
        cost_estimate=pl.CostEstimate(flops=9 * 10**9, bytes_accessed=20 * 2**20, transcendentals=10**6),
    )(tokens, noise[0].T, cotangent.T, mean.T, hess.T, momentum.T)
    return (new_mean.T, new_hess.T, new_momentum.T, input_grad)


def solution(mesh):
    in_specs = (
        P("rep", "tp"),
        P("rep", None, "tp"),
        P("rep", "tp"),
        P("rep", "tp"),
        P("rep", "tp"),
        P("rep", "tp"),
    )
    out_specs = (P("rep", "tp"), P("rep", "tp"), P("rep", "tp"), P(("rep", "tp"), None))
    return jax.shard_map(shards, mesh=mesh, in_specs=in_specs, out_specs=out_specs, check_vma=False)
```

```python
import jax
import jax.numpy as jnp
from jax import lax
from jax.experimental import pallas as pl
from jax.experimental.pallas import tpu as pltpu
from jax.sharding import PartitionSpec as P

MESH = pl.DeviceIdType.MESH
BF, F32 = jnp.bfloat16, jnp.float32

NZ, NY = 4, 4
UNITS, BLOCK, WIDE = 688, 512, 2048
HALF = 256
CHUNKS = ((0, 128), (128, 128), (256, 128), (384, 128), (512, 128), (640, 48))
LAST = len(CHUNKS) - 1
PIECES = 2
PW = WIDE // PIECES
PH = PW // 2
X_FIRST = ((0, 1),)
N_SEM = 192
ORDER = (
    ("noise", 10), ("state", 0), ("state", 1), ("state", 2), ("state_up", 0), ("state_dn", 0), ("token", 0),
    ("token", 1), ("state_up", 1), ("state_dn", 1), ("token_up", 0), ("token_dn", 0), ("state", 3), ("state_up", 2),
    ("state_dn", 2), ("token_up", 1), ("token_dn", 1), ("state", 4), ("token_up", 2), ("noise", 11), ("token_dn", 2),
    ("state_up", 3), ("state_dn", 3), ("noise", 12), ("tokens", 0), ("A", 0), ("A", 1), ("state", 5), ("state_up", 4),
    ("state_dn", 4), ("noise", 14), ("A", 2), ("state_dn", 5), ("state_up", 5), ("B", 0), ("B", 1), ("noise", 16),
    ("B", 2), ("turn", 0), ("C", 0), ("noise", 17), ("turn", 1), ("C", 1), ("noise", 19), ("on_up", 0), ("A", 3),
    ("on_dn", 0), ("turn", 2), ("C", 2), ("noise", 20), ("on_up", 1), ("on_dn", 1), ("noise", 21), ("update", 0),
    ("noise", 24), ("on_up", 2), ("B", 3), ("on_dn", 2), ("A", 4), ("update", 1), ("update", 2), ("A", 5),
    ("turn", 3), ("C", 3), ("B", 4), ("B", 5), ("prod_send", 0, 0), ("prod_send", 0, 1), ("prod_own", 0, 0),
    ("prod_own", 0, 1), ("y", 0, 0), ("x_first", 0, 1), ("turn", 4), ("C", 4), ("turn", 5), ("prod_send", 1, 0),
    ("prod_send", 1, 1), ("C", 5), ("on_dn", 3), ("prod_own", 1, 0), ("y_up", 0, 0), ("y_dn", 0, 0),
    ("prod_own", 1, 1), ("on_up", 3), ("y", 1, 0), ("y", 1, 1), ("y", 0, 1), ("last", 0, 0), ("on_up", 4),
    ("on_dn", 4), ("y_up", 1, 0), ("y_dn", 1, 0), ("on_up", 5), ("on_dn", 5), ("end", 0, 0), ("y_up", 1, 1),
    ("y_dn", 1, 1), ("update", 3), ("y_up", 0, 1), ("y_dn", 0, 1), ("last", 1, 0), ("update", 4), ("last", 1, 1),
    ("update", 5), ("last_own", 0, 1), ("end", 1, 0), ("end", 1, 1),
)
PARTS = 2


def kernel(
    tok_in, noise_in, cot_in, mean_in, hess_in, mom_in,
    mean_out, hess_out, mom_out, din_out,
    tok, tokt, n_own, n_par, ms, wt, cot, mean_v, hess_v, mom_v,
    pre_own, p_send, p_recv, dp, dpt,
    up_send, up_recv, dn_send, dn_recv, up2_send, up2_recv, dn2_send, dn2_recv, g_keep, g_own,
    c_send, c_recv, c_own, yu_send, yu_recv, yd_send, yd_recv, yu2_send, yu2_recv, yd2_send, yd2_recv,
    x_send, x_recv, f_send, f_recv, f_own, o_buf,
    ssem, rsem, lsem,
):
    rep, tp = lax.axis_index("rep"), lax.axis_index("tp")
    z, h = rep // 2, rep % 2
    y, l, c = tp // 4, (tp // 2) % 2, tp % 2

    def at(z=z, h=h, y=y, l=l, c=c):
        return (z * 2 + h, (y * 2 + l) * 2 + c)

    def zz(k):
        return lax.rem(z + k, NZ)

    def yy(k):
        return lax.rem(y + k, NY)

    partner, other_core, other_l = at(h=1 - h), at(c=1 - c), at(l=1 - l)
    z_up, z_dn, y_up, y_dn = at(z=zz(1)), at(z=zz(3)), at(y=yy(1)), at(y=yy(3))
    count = [2]
    sent = []

    def remote(src, dst, device, slot, rslot):
        return pltpu.make_async_remote_copy(
            src_ref=src, dst_ref=dst, send_sem=ssem.at[slot], recv_sem=rsem.at[rslot],
            device_id=device, device_id_type=MESH,
        )

    def send(src, dst, device, start=True):
        slot = count[0]
        count[0] += 1
        copy = remote(src, dst, device, slot, slot)
        if start:
            copy.start()
        sent.append(copy)
        return copy

    peers = [other_l, partner, at(h=1 - h, l=1 - l), other_core, z_up, z_dn, y_up, y_dn]
    barrier = pltpu.get_barrier_semaphore()
    for peer in peers:
        pl.semaphore_signal(barrier, inc=1, device_id=peer, device_id_type=MESH)

    loads = []

    def load(src, dst):
        copy = pltpu.make_async_copy(src, dst, lsem.at[len(loads)])
        copy.start()
        loads.append(copy)
        return copy

    load_mean, load_hess = load(mean_in, mean_v), load(hess_in, hess_v)
    pl.semaphore_wait(barrier, len(peers))

    def tok_slot(s, at_y):
        return tok.at[s, :, pl.ds(pl.multiple_of(at_y * 512 + c * 256, 256), 256)]

    t_near = remote(tok_in, tok_slot(h, y), at(h=l, l=1 - l), 0, h)
    t_near.start()
    t_far = remote(tok_in, tok_slot(h, y), partner, 1, h)
    t_self = pltpu.make_async_copy(tok_in, tok_slot(h, y), rsem.at[h])
    stays = h == l

    @pl.when(stays)
    def _():
        t_self.start()

    @pl.when(jnp.logical_not(stays))
    def _():
        t_far.start()

    n_copies = []

    def send_noise(upto, start=True):
        for n in range(len(n_copies), min(upto, NZ * len(CHUNKS))):
            (first, rows), b = CHUNKS[n // NZ], n % NZ
            n_copies.append(
                send(
                    noise_in.at[pl.ds(first, rows), pl.ds(pl.multiple_of((2 * b + 1 - h) * BLOCK, BLOCK), BLOCK)],
                    n_par.at[pl.ds(first, rows), pl.ds(b * BLOCK, BLOCK)],
                    partner,
                    start,
                )
            )

    send_noise(ORDER[0][1])
    load_own = [
        load(
            noise_in.at[:, pl.ds(pl.multiple_of((2 * b + h) * BLOCK, BLOCK), BLOCK)],
            n_own.at[:, pl.ds(b * BLOCK, BLOCK)],
        )
        for b in range(NZ)
    ]
    load_cot, load_mom = load(cot_in, cot), load(mom_in, mom_v)

    def z_block(k):
        return pl.ds(pl.multiple_of(zz(k) * BLOCK, BLOCK), BLOCK)

    own_z = z_block(0)
    s_up, s_dn, s_up2, s_dn2 = {}, {}, {}, {}

    def state(k):
        first, rows = CHUNKS[k]

        @pl.loop(0, rows // 16)
        def _(i):
            r = pl.ds(pl.multiple_of(first + i * 16, 16), 16)
            ms[0, r, own_z] = mean_v[r, :].astype(BF)
            ms[1, r, own_z] = lax.rsqrt(4.0 * (hess_v[r, :] + 0.001)).astype(BF)

        part = ms.at[:, pl.ds(first, rows), own_z]
        s_up[k], s_dn[k] = send(part, part, z_up), send(part, part, z_dn)

    def state_up(k):
        s_up[k].wait_recv()
        part = ms.at[0, pl.ds(*CHUNKS[k]), z_block(3)]
        s_up2[k] = send(part, part, z_up)

    def state_dn(k):
        s_dn[k].wait_recv()
        part = ms.at[1, pl.ds(*CHUNKS[k]), z_block(1)]
        s_dn2[k] = send(part, part, z_dn)

    load_mean.wait()
    load_hess.wait()

    t_up, t_dn, core = {}, {}, []

    def token(k):
        s = 1 - h if k else h
        slot = tok_slot(s, y)
        pltpu.make_async_copy(slot, slot, rsem.at[s]).wait()
        t_up[k] = send(slot, slot, y_up)
        t_dn[k] = send(slot, slot, y_dn)
        core.append(send(slot, slot, other_core))

    def token_up(k):
        t_up[k].wait_recv()
        slot = tok_slot(1 - h if k == 1 else h, yy(2 if k == 2 else 3))
        core.append(send(slot, slot, other_core))
        if k == 0:
            t_up[2] = send(slot, slot, y_up)

    def token_dn(k):
        t_dn[k].wait_recv()
        slot = tok_slot(h if k == 0 else 1 - h, yy(2 if k == 2 else 1))
        core.append(send(slot, slot, other_core))
        if k == 1:
            t_dn[2] = send(slot, slot, y_dn)

    def tokens(_):
        for copy in core:
            copy.wait_recv()

        @pl.loop(0, 2 * WIDE // 256)
        def _(i):
            s, b = i // 8, i % 8
            f = pl.ds(pl.multiple_of(b * 256, 256), 256)
            tokt[s, f, :] = tok[s, :, f].T

        load_cot.wait()
        for copy in load_own:
            copy.wait()

    p_copies, d_copies = {}, {}

    def weights_and_pre(k):
        first, rows = CHUNKS[k]
        span = pl.ds(first, rows)
        for copy in (s_up2[k], s_dn2[k], *n_copies[NZ * k : NZ * k + NZ]):
            copy.wait_recv()

        @pl.loop(0, rows // 16)
        def _(i):
            r = pl.ds(pl.multiple_of(first + i * 16, 16), 16)
            for b in range(NZ):
                f = pl.ds(b * BLOCK, BLOCK)
                m, g = ms[0, r, f].astype(F32), ms[1, r, f].astype(F32)
                wt[0, r, f] = (m + g * n_own[r, f].astype(F32)).astype(BF)
                wt[1, r, f] = (m + g * n_par[r, f].astype(F32)).astype(BF)

        for half in range(2):
            t = pl.ds(half * HALF, HALF)
            p_send[span, t] = jnp.dot(wt[1, span, :], tokt[1 - h, :, t], preferred_element_type=F32).astype(BF)
        p_copies[k] = send(p_send.at[span], p_recv.at[span], partner)
        for half in range(2):
            t = pl.ds(half * HALF, HALF)
            pre_own[span, t] = jnp.dot(wt[0, span, :], tokt[h, :, t], preferred_element_type=F32)

    def turn(s, k):
        span = pl.ds(*CHUNKS[k])
        for t in range(16):
            if t % 4 == 0:
                turned = dp[s, span, t * 32 : t * 32 + 128].T
            dpt[s, t % 2, pl.ds(t // 2 * 32, 32), span] = turned[t % 4 * 32 : t % 4 * 32 + 32, :]

    def dpre(k):
        first, rows = CHUNKS[k]
        span = pl.ds(first, rows)
        p_copies[k].wait_recv()

        @pl.loop(0, rows // 16)
        def _(i):
            r = pl.ds(pl.multiple_of(first + i * 16, 16), 16)
            pre = pre_own[r, :] + p_recv[r, :].astype(F32)
            sig = 1.0 / (1.0 + jnp.exp(-pre))
            dp[0, r, :] = (cot[r, :].astype(F32) * sig * (1.0 + pre * (1.0 - sig))).astype(BF)

        d_copies[k] = send(dp.at[0, span], dp.at[1, span], partner)
        turn(0, k)

    g_up, g_dn, g_up2, g_dn2 = {}, {}, {}, {}

    came = set()

    def dpre_here(k):
        if k not in came:
            d_copies[k].wait_recv()
            came.add(k)

    def turn_other(k):
        dpre_here(k)
        turn(1, k)

    def grads(k):
        dpre_here(k)
        span = pl.ds(*CHUNKS[k])
        for step in (2, 1, 3, 0):
            for half in range(2):
                t = pl.ds(half * HALF, HALF)
                f = pl.ds(pl.multiple_of(zz(step) * BLOCK + half * HALF, HALF), HALF)
                one = jnp.dot(dp[0, span, :], tok[h, :, f], preferred_element_type=F32)
                two = jnp.dot(dp[1, span, :], tok[1 - h, :, f], preferred_element_type=F32)
                grad, hest = one + two, one * n_own[span, f].astype(F32) + two * n_par[span, f].astype(F32)
                if step == 2:
                    up_send[0, span, t] = grad.astype(BF)
                    dn_send[0, span, t] = hest.astype(BF)
                elif step == 1:
                    g_keep[0, span, t] = grad
                    up_send[1, span, t] = hest.astype(BF)
                elif step == 3:
                    dn_send[1, span, t] = grad.astype(BF)
                    g_keep[1, span, t] = hest
                else:
                    g_own[0, span, t] = grad
                    g_own[1, span, t] = hest
            if step == 1:
                g_up[k] = send(up_send.at[:, span], up_recv.at[:, span], z_up)
            elif step == 3:
                g_dn[k] = send(dn_send.at[:, span], dn_recv.at[:, span], z_dn)

    def on_up(k):
        span = pl.ds(*CHUNKS[k])
        g_up[k].wait_recv()
        up2_send[span, :] = (g_keep[0, span, :] + up_recv[0, span, :].astype(F32)).astype(BF)
        g_up2[k] = send(up2_send.at[span], up2_recv.at[span], z_up)

    def on_dn(k):
        span = pl.ds(*CHUNKS[k])
        g_dn[k].wait_recv()
        dn2_send[span, :] = (g_keep[1, span, :] + dn_recv[0, span, :].astype(F32)).astype(BF)
        g_dn2[k] = send(dn2_send.at[span], dn2_recv.at[span], z_dn)

    stores = []

    def store(src, dst):
        copy = pltpu.make_async_copy(src, dst, lsem.at[len(loads) + len(stores)])
        copy.start()
        stores.append(copy)

    def update(k):
        first, rows = CHUNKS[k]
        if k == 0:
            load_mom.wait()
        span = pl.ds(first, rows)
        g_up2[k].wait_recv()
        g_dn2[k].wait_recv()

        @pl.loop(0, rows // 16)
        def _(i):
            r = pl.ds(pl.multiple_of(first + i * 16, 16), 16)
            mean, hess = mean_v[r, :], hess_v[r, :]
            grad_mean = (g_own[0, r, :] + dn_recv[1, r, :].astype(F32) + up2_recv[r, :].astype(F32)) / 8.0
            hest = (g_own[1, r, :] + up_recv[1, r, :].astype(F32) + dn2_recv[r, :].astype(F32)) / 8.0
            hess_mean = hest / ms[1, r, own_z].astype(F32)
            new_momentum = 0.9 * mom_v[r, :] + 0.1 * grad_mean
            diff = hess - hess_mean
            new_hess = hess + 0.2 * (hess_mean - hess) + 0.5 * 0.04 * diff * diff / (hess + 0.001)
            mom_v[r, :] = new_momentum
            hess_v[r, :] = new_hess
            mean_v[r, :] = mean - 0.5 * (new_momentum + 0.001 * mean) / (new_hess + 0.001)

        store(mean_v.at[span], mean_out.at[span])
        store(hess_v.at[span], hess_out.at[span])
        store(mom_v.at[span], mom_out.at[span])

    c_copies, y_up1, y_dn1, y_up2, y_dn2, f_copies = {}, {}, {}, {}, {}, {}

    def din_product(s, p, keep):
        f = pl.ds(p * PW, PW)
        for q in range(PW // HALF):
            g = pl.ds(p * PW + q * HALF, HALF)
            part = jnp.dot(dpt[s, c if keep else 1 - c], wt[s, :, g], preferred_element_type=F32)
            if keep:
                c_own[s, :, g] = part
            else:
                c_send[s, :, g] = part.astype(BF)
        if not keep:
            c_copies[s, p] = send(c_send.at[s, :, f], c_recv.at[s, :, f], other_core)

    x_copies = {}

    def din_x_first(s, p):
        c_copies[s, p].wait_recv()
        f = pl.ds(p * PW, PW)
        for k in range(NY):
            rows = pl.ds(pl.multiple_of(k * 64 + (1 - l) * 32, 32), 32)
            x_send[pl.ds(k * 32, 32), :] = (c_own[s, rows, f] + c_recv[s, rows, f].astype(F32)).astype(BF)
        x_copies[s, p] = send(x_send, x_recv, other_l)

    def depth(s, p):
        return 32 if (s, p) in X_FIRST else 64

    def din_sum(s, p, k, second):
        g = pl.ds(p * PW + second * PH, PH)
        if (s, p) in X_FIRST:
            rows = pl.ds(pl.multiple_of(yy(k) * 64 + l * 32, 32), 32)
            there = pl.ds(pl.multiple_of(yy(k) * 32, 32), 32)
            return c_own[s, rows, g] + (
                c_recv[s, rows, g].astype(F32) + x_recv[there, pl.ds(second * PH, PH)].astype(F32)
            )
        rows = pl.ds(pl.multiple_of(yy(k) * 64, 64), 64)
        return c_own[s, rows, g] + c_recv[s, rows, g].astype(F32)

    def din_y(s, p):
        (x_copies if (s, p) in X_FIRST else c_copies)[s, p].wait_recv()
        d = pl.ds(0, depth(s, p))
        yu_send[s, p, 0, d] = din_sum(s, p, 2, 0).astype(BF)
        yu_send[s, p, 1, d] = din_sum(s, p, 1, 1).astype(BF)
        y_up1[s, p] = send(yu_send.at[s, p, :, d], yu_recv.at[s, p, :, d], y_up)
        yd_send[s, p, 0, d] = din_sum(s, p, 2, 1).astype(BF)
        yd_send[s, p, 1, d] = din_sum(s, p, 3, 0).astype(BF)
        y_dn1[s, p] = send(yd_send.at[s, p, :, d], yd_recv.at[s, p, :, d], y_dn)

    def din_y_up(s, p):
        d = pl.ds(0, depth(s, p))
        y_up1[s, p].wait_recv()
        yu2_send[s, p, d] = (din_sum(s, p, 1, 0) + yu_recv[s, p, 0, d].astype(F32)).astype(BF)
        y_up2[s, p] = send(yu2_send.at[s, p, d], yu2_recv.at[s, p, d], y_up)

    def din_y_dn(s, p):
        d = pl.ds(0, depth(s, p))
        y_dn1[s, p].wait_recv()
        yd2_send[s, p, d] = (din_sum(s, p, 3, 1) + yd_recv[s, p, 0, d].astype(F32)).astype(BF)
        y_dn2[s, p] = send(yd2_send.at[s, p, d], yd2_recv.at[s, p, d], y_dn)

    def din_last_own(s, p):
        y_up2[s, p].wait_recv()
        y_dn2[s, p].wait_recv()
        d = pl.ds(0, depth(s, p))
        for second in range(2):
            part = din_sum(s, p, 0, second)
            if second:
                part = part + yu_recv[s, p, 1, d].astype(F32) + yd2_recv[s, p, d].astype(F32)
            else:
                part = part + yd_recv[s, p, 1, d].astype(F32) + yu2_recv[s, p, d].astype(F32)
            for b in range(PH // BLOCK):
                block = (p * PW + second * PH) // BLOCK + b
                there = pl.ds(pl.multiple_of((2 * block + h) * BLOCK, BLOCK), BLOCK)
                o_buf[:, there] = part[:, b * BLOCK : (b + 1) * BLOCK].astype(BF)

    def din_last(s, p):
        y_up2[s, p].wait_recv()
        y_dn2[s, p].wait_recv()
        f = pl.ds(p * PW, PW)
        f_copies[s, p] = []
        for near in (False, True):
            which = l if near else 1 - l
            mine = pl.ds(pl.multiple_of(y * 64 + which * 32, 32), 32)
            rows = pl.ds(pl.multiple_of(which * 32, 32), 32)
            for second in range(2):
                g = pl.ds(p * PW + second * PH, PH)
                part = c_own[s, mine, g] + c_recv[s, mine, g].astype(F32)
                if second:
                    part = part + yu_recv[s, p, 1, rows, :].astype(F32) + yd2_recv[s, p, rows, :].astype(F32)
                else:
                    part = part + yd_recv[s, p, 1, rows, :].astype(F32) + yu2_recv[s, p, rows, :].astype(F32)
                if near and not s:
                    f_own[:, g] = part
                else:
                    f_send[s + near, :, g] = part.astype(BF)
            if s or not near:
                there = partner if near else at(h=1 - h, l=1 - l) if s else other_l
                f_copies[s, p].append(send(f_send.at[s + near, :, f], f_recv.at[s + near, :, f], there))

    def din_end(s, p):
        for copy in f_copies[s, p]:
            copy.wait_recv()
        for b in range(p * PW // BLOCK, (p + 1) * PW // BLOCK):
            f = pl.ds(b * BLOCK, BLOCK)
            there = pl.ds(pl.multiple_of((2 * b + (1 - h if s else h)) * BLOCK, BLOCK), BLOCK)
            if s:
                part = f_recv[1, :, f].astype(F32) + f_recv[2, :, f].astype(F32)
            else:
                part = f_own[:, f] + f_recv[0, :, f].astype(F32)
            o_buf[:, there] = part.astype(BF)

    steps = {
        "noise": send_noise, "state": state, "state_up": state_up, "state_dn": state_dn,
        "token": token, "token_up": token_up, "token_dn": token_dn, "tokens": tokens,
        "A": weights_and_pre, "B": dpre, "turn": turn_other, "C": grads,
        "on_up": on_up, "on_dn": on_dn, "update": update,
        "prod_send": lambda s, p: din_product(s, p, False), "prod_own": lambda s, p: din_product(s, p, True),
        "x_first": din_x_first, "y": din_y, "y_up": din_y_up, "y_dn": din_y_dn,
        "last": din_last, "last_own": din_last_own, "end": din_end,
    }
    for name, *where in ORDER:
        steps[name](*where)
    store(o_buf, din_out)
    for copy in stores:
        copy.wait()
    t_near.wait_send()

    @pl.when(jnp.logical_not(stays))
    def _():
        t_far.wait_send()

    for copy in sent:
        copy.wait_send()


def settle(*refs):
    n = len(refs) // 2
    for src, dst in zip(refs[:n], refs[n:]):
        dst[...] = src[...]


def shards(tokens, noise, cotangent, mean, hess, momentum):
    vm = pltpu.VMEM
    units = (UNITS, BLOCK)
    piece = (2, PIECES, 64, PH)
    scratch = [
        vm((2, BLOCK, WIDE), BF),
        vm((2, WIDE, BLOCK), BF),
        vm((UNITS, WIDE), BF),
        vm((UNITS, WIDE), BF),
        vm((2, UNITS, WIDE), BF),
        vm((2, UNITS, WIDE), BF),
        vm(units, BF),
        vm(units, F32),
        vm(units, F32),
        vm(units, F32),
        vm(units, F32),
        vm(units, BF),
        vm(units, BF),
        vm((2,) + units, BF),
        vm((2, 2, HALF, UNITS), BF),
        *[vm((2,) + units, BF)] * 4,
        *[vm(units, BF)] * 4,
        vm((2,) + units, F32),
        vm((2,) + units, F32),
        vm((2, HALF, WIDE), BF),
        vm((2, HALF, WIDE), BF),
        vm((2, HALF, WIDE), F32),
        *[vm((2, PIECES, 2, 64, PH), BF)] * 4,
        *[vm(piece, BF)] * 4,
        vm((128, PW), BF),
        vm((128, PW), BF),
        vm((3, 32, WIDE), BF),
        vm((3, 32, WIDE), BF),
        vm((32, WIDE), F32),
        vm((32, 2 * WIDE), BF),
        pltpu.SemaphoreType.DMA((N_SEM,)),
        pltpu.SemaphoreType.DMA((N_SEM,)),
        pltpu.SemaphoreType.DMA((32,)),
    ]
    anywhere = pl.BlockSpec(memory_space=pl.ANY)
    outs = [jax.ShapeDtypeStruct(units, F32)] * 3 + [jax.ShapeDtypeStruct((32, 2 * WIDE), BF)]
    results = pl.pallas_call(
        kernel,
        out_shape=outs,
        in_specs=[anywhere] * 6,
        out_specs=[anywhere] * 4,
        scratch_shapes=scratch,
        compiler_params=pltpu.CompilerParams(
            collective_id=1, has_side_effects=True, vmem_limit_bytes=63 << 20
        ),
        cost_estimate=pl.CostEstimate(flops=9 * 10**9, bytes_accessed=20 * 2**20, transcendentals=10**6),
    )(tokens, noise[0].T, cotangent.T, mean.T, hess.T, momentum.T)
    blocks = [pl.BlockSpec((o.shape[0] // PARTS, o.shape[1]), lambda i: (i, 0)) for o in outs]
    new_mean, new_hess, new_momentum, input_grad = pl.pallas_call(
        settle,
        grid=(PARTS,),
        out_shape=outs,
        in_specs=blocks,
        out_specs=blocks,
        compiler_params=pltpu.CompilerParams(vmem_limit_bytes=63 << 20),
        cost_estimate=pl.CostEstimate(flops=0, bytes_accessed=9 * 2**20, transcendentals=0),
    )(*results)
    return (new_mean.T, new_hess.T, new_momentum.T, input_grad)


def solution(mesh):
    in_specs = (
        P("rep", "tp"),
        P("rep", None, "tp"),
        P("rep", "tp"),
        P("rep", "tp"),
        P("rep", "tp"),
        P("rep", "tp"),
    )
    out_specs = (P("rep", "tp"), P("rep", "tp"), P("rep", "tp"), P(("rep", "tp"), None))
    return jax.shard_map(shards, mesh=mesh, in_specs=in_specs, out_specs=out_specs, check_vma=False)
```

```python
import jax
import jax.numpy as jnp
from jax import lax
from jax.experimental import pallas as pl
from jax.experimental.pallas import tpu as pltpu
from jax.sharding import PartitionSpec as P

MESH = pl.DeviceIdType.MESH
BF, F32 = jnp.bfloat16, jnp.float32

NZ, NY = 4, 4
UNITS, BLOCK, WIDE = 688, 512, 2048
HALF = 256
CHUNKS = ((0, 128), (128, 128), (256, 128), (384, 128), (512, 128), (640, 48))
LAST = len(CHUNKS) - 1
PIECES = 4
PW = WIDE // PIECES
PH = PW // 2
X_FIRST = ((0, 3),)
N_SEM = 192
ORDER = (
    ("noise", 10), ("state", 0), ("state", 1), ("state", 2), ("state", 3), ("state_up", 0), ("state_dn", 0),
    ("token", 0), ("token", 1), ("state_up", 1), ("state_dn", 1), ("token_up", 0), ("token_dn", 0), ("state", 4),
    ("state_up", 2), ("state_dn", 2), ("token_up", 1), ("token_dn", 1), ("state_up", 3), ("state_dn", 3),
    ("token_up", 2), ("state", 5), ("noise", 11), ("token_dn", 2), ("noise", 12), ("tokens", 0), ("noise", 13),
    ("A", 0), ("A", 1), ("state_up", 4), ("state_dn", 4), ("noise", 14), ("A", 2), ("state_up", 5), ("state_dn", 5),
    ("noise", 15), ("B", 0), ("B", 1), ("noise", 16), ("B", 2), ("noise", 17), ("turn", 0), ("C", 0), ("noise", 18),
    ("turn", 1), ("C", 1), ("noise", 19), ("A", 3), ("on_up", 0), ("turn", 2), ("C", 2), ("on_dn", 0), ("noise", 21),
    ("on_up", 1), ("on_dn", 1), ("noise", 24), ("B", 3), ("on_dn", 2), ("A", 4), ("on_up", 2), ("update", 0),
    ("update", 1), ("A", 5), ("turn", 3), ("C", 3), ("update", 2), ("B", 4), ("B", 5), ("prod_send", 0, 0),
    ("prod_send", 0, 1), ("prod_send", 0, 2), ("prod_send", 0, 3), ("prod_own", 0, 0), ("prod_own", 0, 1),
    ("prod_own", 0, 2), ("prod_own", 0, 3), ("y", 0, 0), ("y", 0, 1), ("y", 0, 2), ("x_first", 0, 3), ("turn", 4),
    ("on_up", 3), ("C", 4), ("turn", 5), ("y_up", 0, 0), ("y_dn", 0, 0), ("prod_send", 1, 0), ("prod_send", 1, 1),
    ("prod_send", 1, 2), ("y_up", 0, 1), ("y_dn", 0, 1), ("prod_send", 1, 3), ("prod_own", 1, 0), ("prod_own", 1, 1),
    ("y", 0, 3), ("y_dn", 0, 2), ("y_up", 0, 2), ("y", 1, 0), ("last", 0, 0), ("y", 1, 1), ("prod_own", 1, 2),
    ("last", 0, 1), ("y", 1, 2), ("prod_own", 1, 3), ("y", 1, 3), ("y_dn", 0, 3), ("y_up", 0, 3), ("on_dn", 3),
    ("C", 5), ("last", 0, 2), ("end", 0, 0), ("on_dn", 4), ("end", 0, 1), ("y_up", 1, 0), ("y_dn", 1, 0),
    ("on_up", 4), ("y_up", 1, 1), ("y_dn", 1, 1), ("end", 0, 2), ("y_up", 1, 2), ("y_dn", 1, 2), ("on_up", 5),
    ("update", 3), ("y_up", 1, 3), ("y_dn", 1, 3), ("last_own", 0, 3), ("last", 1, 0), ("on_dn", 5), ("last", 1, 1),
    ("last", 1, 2), ("last", 1, 3), ("end", 1, 0), ("update", 4), ("end", 1, 1), ("update", 5), ("end", 1, 2),
    ("end", 1, 3),
)
PARTS = 2


def kernel(
    tok_in, noise_in, cot_in, mean_in, hess_in, mom_in,
    mean_out, hess_out, mom_out, din_out,
    tok, tokt, n_own, n_par, ms, wt, cot, mean_v, hess_v, mom_v,
    pre_own, p_send, p_recv, dp, dpt,
    up_send, up_recv, dn_send, dn_recv, up2_send, up2_recv, dn2_send, dn2_recv, g_keep, g_own,
    c_send, c_recv, c_own, yu_send, yu_recv, yd_send, yd_recv, yu2_send, yu2_recv, yd2_send, yd2_recv,
    x_send, x_recv, f_send, f_recv, f_own, o_buf,
    ssem, rsem, lsem,
):
    rep, tp = lax.axis_index("rep"), lax.axis_index("tp")
    z, h = rep // 2, rep % 2
    y, l, c = tp // 4, (tp // 2) % 2, tp % 2

    def at(z=z, h=h, y=y, l=l, c=c):
        return (z * 2 + h, (y * 2 + l) * 2 + c)

    def zz(k):
        return lax.rem(z + k, NZ)

    def yy(k):
        return lax.rem(y + k, NY)

    partner, other_core, other_l = at(h=1 - h), at(c=1 - c), at(l=1 - l)
    z_up, z_dn, y_up, y_dn = at(z=zz(1)), at(z=zz(3)), at(y=yy(1)), at(y=yy(3))
    count = [2]
    sent = []

    def remote(src, dst, device, slot, rslot):
        return pltpu.make_async_remote_copy(
            src_ref=src, dst_ref=dst, send_sem=ssem.at[slot], recv_sem=rsem.at[rslot],
            device_id=device, device_id_type=MESH,
        )

    def send(src, dst, device, start=True):
        slot = count[0]
        count[0] += 1
        copy = remote(src, dst, device, slot, slot)
        if start:
            copy.start()
        sent.append(copy)
        return copy

    peers = [other_l, partner, at(h=1 - h, l=1 - l), other_core, z_up, z_dn, y_up, y_dn]
    barrier = pltpu.get_barrier_semaphore()
    for peer in peers:
        pl.semaphore_signal(barrier, inc=1, device_id=peer, device_id_type=MESH)

    loads = []

    def load(src, dst):
        copy = pltpu.make_async_copy(src, dst, lsem.at[len(loads)])
        copy.start()
        loads.append(copy)
        return copy

    load_mean, load_hess = load(mean_in, mean_v), load(hess_in, hess_v)
    pl.semaphore_wait(barrier, len(peers))

    def tok_slot(s, at_y):
        return tok.at[s, :, pl.ds(pl.multiple_of(at_y * 512 + c * 256, 256), 256)]

    t_near = remote(tok_in, tok_slot(h, y), at(h=l, l=1 - l), 0, h)
    t_near.start()
    t_far = remote(tok_in, tok_slot(h, y), partner, 1, h)
    t_self = pltpu.make_async_copy(tok_in, tok_slot(h, y), rsem.at[h])
    stays = h == l

    @pl.when(stays)
    def _():
        t_self.start()

    @pl.when(jnp.logical_not(stays))
    def _():
        t_far.start()

    n_copies = []

    def send_noise(upto, start=True):
        for n in range(len(n_copies), min(upto, NZ * len(CHUNKS))):
            (first, rows), b = CHUNKS[n // NZ], n % NZ
            n_copies.append(
                send(
                    noise_in.at[pl.ds(first, rows), pl.ds(pl.multiple_of((2 * b + 1 - h) * BLOCK, BLOCK), BLOCK)],
                    n_par.at[pl.ds(first, rows), pl.ds(b * BLOCK, BLOCK)],
                    partner,
                    start,
                )
            )

    send_noise(ORDER[0][1])
    load_own = [
        load(
            noise_in.at[:, pl.ds(pl.multiple_of((2 * b + h) * BLOCK, BLOCK), BLOCK)],
            n_own.at[:, pl.ds(b * BLOCK, BLOCK)],
        )
        for b in range(NZ)
    ]
    load_cot, load_mom = load(cot_in, cot), load(mom_in, mom_v)

    def z_block(k):
        return pl.ds(pl.multiple_of(zz(k) * BLOCK, BLOCK), BLOCK)

    own_z = z_block(0)
    s_up, s_dn, s_up2, s_dn2 = {}, {}, {}, {}

    def state(k):
        first, rows = CHUNKS[k]

        @pl.loop(0, rows // 16)
        def _(i):
            r = pl.ds(pl.multiple_of(first + i * 16, 16), 16)
            ms[0, r, own_z] = mean_v[r, :].astype(BF)
            ms[1, r, own_z] = lax.rsqrt(4.0 * (hess_v[r, :] + 0.001)).astype(BF)

        part = ms.at[:, pl.ds(first, rows), own_z]
        s_up[k], s_dn[k] = send(part, part, z_up), send(part, part, z_dn)

    def state_up(k):
        s_up[k].wait_recv()
        part = ms.at[0, pl.ds(*CHUNKS[k]), z_block(3)]
        s_up2[k] = send(part, part, z_up)

    def state_dn(k):
        s_dn[k].wait_recv()
        part = ms.at[1, pl.ds(*CHUNKS[k]), z_block(1)]
        s_dn2[k] = send(part, part, z_dn)

    load_mean.wait()
    load_hess.wait()

    t_up, t_dn, core = {}, {}, []

    def token(k):
        s = 1 - h if k else h
        slot = tok_slot(s, y)
        pltpu.make_async_copy(slot, slot, rsem.at[s]).wait()
        t_up[k] = send(slot, slot, y_up)
        t_dn[k] = send(slot, slot, y_dn)
        core.append(send(slot, slot, other_core))

    def token_up(k):
        t_up[k].wait_recv()
        slot = tok_slot(1 - h if k == 1 else h, yy(2 if k == 2 else 3))
        core.append(send(slot, slot, other_core))
        if k == 0:
            t_up[2] = send(slot, slot, y_up)

    def token_dn(k):
        t_dn[k].wait_recv()
        slot = tok_slot(h if k == 0 else 1 - h, yy(2 if k == 2 else 1))
        core.append(send(slot, slot, other_core))
        if k == 1:
            t_dn[2] = send(slot, slot, y_dn)

    def tokens(_):
        for copy in core:
            copy.wait_recv()

        @pl.loop(0, 2 * WIDE // 256)
        def _(i):
            s, b = i // 8, i % 8
            f = pl.ds(pl.multiple_of(b * 256, 256), 256)
            tokt[s, f, :] = tok[s, :, f].T

        load_cot.wait()
        for copy in load_own:
            copy.wait()

    p_copies, d_copies = {}, {}

    def weights_and_pre(k):
        first, rows = CHUNKS[k]
        span = pl.ds(first, rows)
        for copy in (s_up2[k], s_dn2[k], *n_copies[NZ * k : NZ * k + NZ]):
            copy.wait_recv()

        @pl.loop(0, rows // 16)
        def _(i):
            r = pl.ds(pl.multiple_of(first + i * 16, 16), 16)
            for b in range(NZ):
                f = pl.ds(b * BLOCK, BLOCK)
                m, g = ms[0, r, f].astype(F32), ms[1, r, f].astype(F32)
                wt[0, r, f] = (m + g * n_own[r, f].astype(F32)).astype(BF)
                wt[1, r, f] = (m + g * n_par[r, f].astype(F32)).astype(BF)

        for half in range(2):
            t = pl.ds(half * HALF, HALF)
            p_send[span, t] = jnp.dot(wt[1, span, :], tokt[1 - h, :, t], preferred_element_type=F32).astype(BF)
        p_copies[k] = send(p_send.at[span], p_recv.at[span], partner)
        for half in range(2):
            t = pl.ds(half * HALF, HALF)
            pre_own[span, t] = jnp.dot(wt[0, span, :], tokt[h, :, t], preferred_element_type=F32)

    def turn(s, k):
        span = pl.ds(*CHUNKS[k])
        for t in range(16):
            if t % 4 == 0:
                turned = dp[s, span, t * 32 : t * 32 + 128].T
            dpt[s, t % 2, pl.ds(t // 2 * 32, 32), span] = turned[t % 4 * 32 : t % 4 * 32 + 32, :]

    def dpre(k):
        first, rows = CHUNKS[k]
        span = pl.ds(first, rows)
        p_copies[k].wait_recv()

        @pl.loop(0, rows // 16)
        def _(i):
            r = pl.ds(pl.multiple_of(first + i * 16, 16), 16)
            pre = pre_own[r, :] + p_recv[r, :].astype(F32)
            sig = 1.0 / (1.0 + jnp.exp(-pre))
            dp[0, r, :] = (cot[r, :].astype(F32) * sig * (1.0 + pre * (1.0 - sig))).astype(BF)

        d_copies[k] = send(dp.at[0, span], dp.at[1, span], partner)
        turn(0, k)

    g_up, g_dn, g_up2, g_dn2 = {}, {}, {}, {}

    came = set()

    def dpre_here(k):
        if k not in came:
            d_copies[k].wait_recv()
            came.add(k)

    def turn_other(k):
        dpre_here(k)
        turn(1, k)

    def grads(k):
        dpre_here(k)
        span = pl.ds(*CHUNKS[k])
        for step in (2, 1, 3, 0):
            for half in range(2):
                t = pl.ds(half * HALF, HALF)
                f = pl.ds(pl.multiple_of(zz(step) * BLOCK + half * HALF, HALF), HALF)
                one = jnp.dot(dp[0, span, :], tok[h, :, f], preferred_element_type=F32)
                two = jnp.dot(dp[1, span, :], tok[1 - h, :, f], preferred_element_type=F32)
                grad, hest = one + two, one * n_own[span, f].astype(F32) + two * n_par[span, f].astype(F32)
                if step == 2:
                    up_send[0, span, t] = grad.astype(BF)
                    dn_send[0, span, t] = hest.astype(BF)
                elif step == 1:
                    g_keep[0, span, t] = grad
                    up_send[1, span, t] = hest.astype(BF)
                elif step == 3:
                    dn_send[1, span, t] = grad.astype(BF)
                    g_keep[1, span, t] = hest
                else:
                    g_own[0, span, t] = grad
                    g_own[1, span, t] = hest
            if step == 1:
                g_up[k] = send(up_send.at[:, span], up_recv.at[:, span], z_up)
            elif step == 3:
                g_dn[k] = send(dn_send.at[:, span], dn_recv.at[:, span], z_dn)

    def on_up(k):
        span = pl.ds(*CHUNKS[k])
        g_up[k].wait_recv()
        up2_send[span, :] = (g_keep[0, span, :] + up_recv[0, span, :].astype(F32)).astype(BF)
        g_up2[k] = send(up2_send.at[span], up2_recv.at[span], z_up)

    def on_dn(k):
        span = pl.ds(*CHUNKS[k])
        g_dn[k].wait_recv()
        dn2_send[span, :] = (g_keep[1, span, :] + dn_recv[0, span, :].astype(F32)).astype(BF)
        g_dn2[k] = send(dn2_send.at[span], dn2_recv.at[span], z_dn)

    stores = []

    def store(src, dst):
        copy = pltpu.make_async_copy(src, dst, lsem.at[len(loads) + len(stores)])
        copy.start()
        stores.append(copy)

    def update(k):
        first, rows = CHUNKS[k]
        if k == 0:
            load_mom.wait()
        span = pl.ds(first, rows)
        g_up2[k].wait_recv()
        g_dn2[k].wait_recv()

        @pl.loop(0, rows // 16)
        def _(i):
            r = pl.ds(pl.multiple_of(first + i * 16, 16), 16)
            mean, hess = mean_v[r, :], hess_v[r, :]
            grad_mean = (g_own[0, r, :] + dn_recv[1, r, :].astype(F32) + up2_recv[r, :].astype(F32)) / 8.0
            hest = (g_own[1, r, :] + up_recv[1, r, :].astype(F32) + dn2_recv[r, :].astype(F32)) / 8.0
            hess_mean = hest / ms[1, r, own_z].astype(F32)
            new_momentum = 0.9 * mom_v[r, :] + 0.1 * grad_mean
            diff = hess - hess_mean
            new_hess = hess + 0.2 * (hess_mean - hess) + 0.5 * 0.04 * diff * diff / (hess + 0.001)
            mom_v[r, :] = new_momentum
            hess_v[r, :] = new_hess
            mean_v[r, :] = mean - 0.5 * (new_momentum + 0.001 * mean) / (new_hess + 0.001)

        store(mean_v.at[span], mean_out.at[span])
        store(hess_v.at[span], hess_out.at[span])
        store(mom_v.at[span], mom_out.at[span])

    c_copies, y_up1, y_dn1, y_up2, y_dn2, f_copies = {}, {}, {}, {}, {}, {}

    def din_product(s, p, keep):
        f = pl.ds(p * PW, PW)
        for q in range(PW // HALF):
            g = pl.ds(p * PW + q * HALF, HALF)
            part = jnp.dot(dpt[s, c if keep else 1 - c], wt[s, :, g], preferred_element_type=F32)
            if keep:
                c_own[s, :, g] = part
            else:
                c_send[s, :, g] = part.astype(BF)
        if not keep:
            c_copies[s, p] = send(c_send.at[s, :, f], c_recv.at[s, :, f], other_core)

    x_copies = {}

    def din_x_first(s, p):
        c_copies[s, p].wait_recv()
        at_x = X_FIRST.index((s, p))
        f = pl.ds(p * PW, PW)
        for k in range(NY):
            rows = pl.ds(pl.multiple_of(k * 64 + (1 - l) * 32, 32), 32)
            x_send[at_x, pl.ds(k * 32, 32), :] = (c_own[s, rows, f] + c_recv[s, rows, f].astype(F32)).astype(BF)
        x_copies[s, p] = send(x_send.at[at_x], x_recv.at[at_x], other_l)

    def depth(s, p):
        return 32 if (s, p) in X_FIRST else 64

    def din_sum(s, p, k, second):
        g = pl.ds(p * PW + second * PH, PH)
        if (s, p) in X_FIRST:
            rows = pl.ds(pl.multiple_of(yy(k) * 64 + l * 32, 32), 32)
            there = pl.ds(pl.multiple_of(yy(k) * 32, 32), 32)
            return c_own[s, rows, g] + (
                c_recv[s, rows, g].astype(F32) + x_recv[X_FIRST.index((s, p)), there, pl.ds(second * PH, PH)].astype(F32)
            )
        rows = pl.ds(pl.multiple_of(yy(k) * 64, 64), 64)
        return c_own[s, rows, g] + c_recv[s, rows, g].astype(F32)

    def din_y(s, p):
        (x_copies if (s, p) in X_FIRST else c_copies)[s, p].wait_recv()
        d = pl.ds(0, depth(s, p))
        yu_send[s, p, 0, d] = din_sum(s, p, 2, 0).astype(BF)
        yu_send[s, p, 1, d] = din_sum(s, p, 1, 1).astype(BF)
        y_up1[s, p] = send(yu_send.at[s, p, :, d], yu_recv.at[s, p, :, d], y_up)
        yd_send[s, p, 0, d] = din_sum(s, p, 2, 1).astype(BF)
        yd_send[s, p, 1, d] = din_sum(s, p, 3, 0).astype(BF)
        y_dn1[s, p] = send(yd_send.at[s, p, :, d], yd_recv.at[s, p, :, d], y_dn)

    def din_y_up(s, p):
        d = pl.ds(0, depth(s, p))
        y_up1[s, p].wait_recv()
        yu2_send[s, p, d] = (din_sum(s, p, 1, 0) + yu_recv[s, p, 0, d].astype(F32)).astype(BF)
        y_up2[s, p] = send(yu2_send.at[s, p, d], yu2_recv.at[s, p, d], y_up)

    def din_y_dn(s, p):
        d = pl.ds(0, depth(s, p))
        y_dn1[s, p].wait_recv()
        yd2_send[s, p, d] = (din_sum(s, p, 3, 1) + yd_recv[s, p, 0, d].astype(F32)).astype(BF)
        y_dn2[s, p] = send(yd2_send.at[s, p, d], yd2_recv.at[s, p, d], y_dn)

    def din_last_own(s, p):
        y_up2[s, p].wait_recv()
        y_dn2[s, p].wait_recv()
        d = pl.ds(0, depth(s, p))
        for second in range(2):
            part = din_sum(s, p, 0, second)
            if second:
                part = part + yu_recv[s, p, 1, d].astype(F32) + yd2_recv[s, p, d].astype(F32)
            else:
                part = part + yd_recv[s, p, 1, d].astype(F32) + yu2_recv[s, p, d].astype(F32)
            first = p * PW + second * PH
            there = (2 * (first // BLOCK) + h) * BLOCK + first % BLOCK
            o_buf[:, pl.ds(pl.multiple_of(there, PH), PH)] = part.astype(BF)

    def din_last(s, p):
        y_up2[s, p].wait_recv()
        y_dn2[s, p].wait_recv()
        f = pl.ds(p * PW, PW)
        f_copies[s, p] = []
        for near in (False, True):
            which = l if near else 1 - l
            mine = pl.ds(pl.multiple_of(y * 64 + which * 32, 32), 32)
            rows = pl.ds(pl.multiple_of(which * 32, 32), 32)
            for second in range(2):
                g = pl.ds(p * PW + second * PH, PH)
                part = c_own[s, mine, g] + c_recv[s, mine, g].astype(F32)
                if second:
                    part = part + yu_recv[s, p, 1, rows, :].astype(F32) + yd2_recv[s, p, rows, :].astype(F32)
                else:
                    part = part + yd_recv[s, p, 1, rows, :].astype(F32) + yu2_recv[s, p, rows, :].astype(F32)
                if near and not s:
                    f_own[:, g] = part
                else:
                    f_send[s + near, :, g] = part.astype(BF)
            if s or not near:
                there = partner if near else at(h=1 - h, l=1 - l) if s else other_l
                f_copies[s, p].append(send(f_send.at[s + near, :, f], f_recv.at[s + near, :, f], there))

    def din_end(s, p):
        for copy in f_copies[s, p]:
            copy.wait_recv()
        for b in range(p * PW // BLOCK, (p + 1) * PW // BLOCK):
            f = pl.ds(b * BLOCK, BLOCK)
            there = pl.ds(pl.multiple_of((2 * b + (1 - h if s else h)) * BLOCK, BLOCK), BLOCK)
            if s:
                part = f_recv[1, :, f].astype(F32) + f_recv[2, :, f].astype(F32)
            else:
                part = f_own[:, f] + f_recv[0, :, f].astype(F32)
            o_buf[:, there] = part.astype(BF)

    steps = {
        "noise": send_noise, "state": state, "state_up": state_up, "state_dn": state_dn,
        "token": token, "token_up": token_up, "token_dn": token_dn, "tokens": tokens,
        "A": weights_and_pre, "B": dpre, "turn": turn_other, "C": grads,
        "on_up": on_up, "on_dn": on_dn, "update": update,
        "prod_send": lambda s, p: din_product(s, p, False), "prod_own": lambda s, p: din_product(s, p, True),
        "x_first": din_x_first, "y": din_y, "y_up": din_y_up, "y_dn": din_y_dn,
        "last": din_last, "last_own": din_last_own, "end": din_end,
    }
    for name, *where in ORDER:
        steps[name](*where)
    store(o_buf, din_out)
    for copy in stores:
        copy.wait()
    t_near.wait_send()

    @pl.when(jnp.logical_not(stays))
    def _():
        t_far.wait_send()

    for copy in sent:
        copy.wait_send()


def settle(*refs):
    n = len(refs) // 2
    for src, dst in zip(refs[:n], refs[n:]):
        dst[...] = src[...]


def shards(tokens, noise, cotangent, mean, hess, momentum):
    vm = pltpu.VMEM
    units = (UNITS, BLOCK)
    piece = (2, PIECES, 64, PH)
    scratch = [
        vm((2, BLOCK, WIDE), BF),
        vm((2, WIDE, BLOCK), BF),
        vm((UNITS, WIDE), BF),
        vm((UNITS, WIDE), BF),
        vm((2, UNITS, WIDE), BF),
        vm((2, UNITS, WIDE), BF),
        vm(units, BF),
        vm(units, F32),
        vm(units, F32),
        vm(units, F32),
        vm(units, F32),
        vm(units, BF),
        vm(units, BF),
        vm((2,) + units, BF),
        vm((2, 2, HALF, UNITS), BF),
        *[vm((2,) + units, BF)] * 4,
        *[vm(units, BF)] * 4,
        vm((2,) + units, F32),
        vm((2,) + units, F32),
        vm((2, HALF, WIDE), BF),
        vm((2, HALF, WIDE), BF),
        vm((2, HALF, WIDE), F32),
        *[vm((2, PIECES, 2, 64, PH), BF)] * 4,
        *[vm(piece, BF)] * 4,
        vm((len(X_FIRST), 128, PW), BF),
        vm((len(X_FIRST), 128, PW), BF),
        vm((3, 32, WIDE), BF),
        vm((3, 32, WIDE), BF),
        vm((32, WIDE), F32),
        vm((32, 2 * WIDE), BF),
        pltpu.SemaphoreType.DMA((N_SEM,)),
        pltpu.SemaphoreType.DMA((N_SEM,)),
        pltpu.SemaphoreType.DMA((32,)),
    ]
    anywhere = pl.BlockSpec(memory_space=pl.ANY)
    outs = [jax.ShapeDtypeStruct(units, F32)] * 3 + [jax.ShapeDtypeStruct((32, 2 * WIDE), BF)]
    results = pl.pallas_call(
        kernel,
        out_shape=outs,
        in_specs=[anywhere] * 6,
        out_specs=[anywhere] * 4,
        scratch_shapes=scratch,
        compiler_params=pltpu.CompilerParams(
            collective_id=1, has_side_effects=True, vmem_limit_bytes=63 << 20
        ),
        cost_estimate=pl.CostEstimate(flops=9 * 10**9, bytes_accessed=20 * 2**20, transcendentals=10**6),
    )(tokens, noise[0].T, cotangent.T, mean.T, hess.T, momentum.T)
    blocks = [pl.BlockSpec((o.shape[0] // PARTS, o.shape[1]), lambda i: (i, 0)) for o in outs]
    new_mean, new_hess, new_momentum, input_grad = pl.pallas_call(
        settle,
        grid=(PARTS,),
        out_shape=outs,
        in_specs=blocks,
        out_specs=blocks,
        compiler_params=pltpu.CompilerParams(vmem_limit_bytes=63 << 20),
        cost_estimate=pl.CostEstimate(flops=0, bytes_accessed=9 * 2**20, transcendentals=0),
    )(*results)
    return (new_mean.T, new_hess.T, new_momentum.T, input_grad)


def solution(mesh):
    in_specs = (
        P("rep", "tp"),
        P("rep", None, "tp"),
        P("rep", "tp"),
        P("rep", "tp"),
        P("rep", "tp"),
        P("rep", "tp"),
    )
    out_specs = (P("rep", "tp"), P("rep", "tp"), P("rep", "tp"), P(("rep", "tp"), None))
    return jax.shard_map(shards, mesh=mesh, in_specs=in_specs, out_specs=out_specs, check_vma=False)
```

```python
import jax
import jax.numpy as jnp
from jax import lax
from jax.experimental import pallas as pl
from jax.experimental.pallas import tpu as pltpu
from jax.sharding import PartitionSpec as P

MESH = pl.DeviceIdType.MESH
BF, F32 = jnp.bfloat16, jnp.float32

NZ, NY = 4, 4
UNITS, BLOCK, WIDE = 688, 512, 2048
HALF = 256
CHUNKS = ((0, 128), (128, 128), (256, 128), (384, 128), (512, 128), (640, 48))
LAST = len(CHUNKS) - 1
PIECES = 4
PW = WIDE // PIECES
PH = PW // 2
X_FIRST = ((0, 3),)
N_SEM = 192
ORDER = (
    ("noise", 9), ("state", 0), ("state", 1), ("state", 2), ("state", 3), ("state_up", 0), ("state_dn", 0),
    ("token", 0), ("token", 1), ("state_up", 1), ("state_dn", 1), ("token_up", 0), ("token_dn", 0), ("state", 4),
    ("state_up", 2), ("state_dn", 2), ("token_up", 1), ("token_dn", 1), ("noise", 10), ("state_up", 3),
    ("state_dn", 3), ("noise", 11), ("token_up", 2), ("state", 5), ("noise", 12), ("token_dn", 2), ("noise", 13),
    ("tokens", 0), ("A", 0), ("A", 1), ("state_up", 4), ("state_dn", 4), ("noise", 14), ("A", 2), ("state_up", 5),
    ("state_dn", 5), ("noise", 15), ("B", 0), ("B", 1), ("noise", 16), ("B", 2), ("noise", 17), ("turn", 0), ("C", 0),
    ("noise", 18), ("turn", 1), ("C", 1), ("noise", 19), ("A", 3), ("on_up", 0), ("on_dn", 0), ("turn", 2),
    ("noise", 20), ("C", 2), ("noise", 22), ("on_up", 1), ("noise", 23), ("on_dn", 1), ("noise", 24), ("update", 0),
    ("B", 3), ("A", 4), ("on_dn", 2), ("on_up", 2), ("update", 1), ("A", 5), ("turn", 3), ("C", 3), ("update", 2),
    ("B", 4), ("B", 5), ("prod_send", 0, 0), ("prod_send", 0, 1), ("prod_send", 0, 2), ("prod_send", 0, 3),
    ("prod_own", 0, 0), ("prod_own", 0, 1), ("prod_own", 0, 2), ("prod_own", 0, 3), ("y", 0, 0), ("y", 0, 1),
    ("y", 0, 2), ("x_first", 0, 3), ("on_up", 3), ("turn", 4), ("on_dn", 3), ("C", 4), ("y_up", 0, 0), ("y_dn", 0, 0),
    ("turn", 5), ("prod_send", 1, 0), ("y_up", 0, 1), ("y_dn", 0, 1), ("prod_send", 1, 1), ("prod_send", 1, 2),
    ("prod_send", 1, 3), ("y_up", 0, 2), ("y_dn", 0, 2), ("y", 0, 3), ("prod_own", 1, 0), ("y", 1, 0),
    ("prod_own", 1, 1), ("y", 1, 1), ("prod_own", 1, 2), ("y", 1, 2), ("prod_own", 1, 3), ("y", 1, 3), ("y_up", 0, 3),
    ("y_dn", 0, 3), ("last", 0, 0), ("last", 0, 1), ("last", 0, 2), ("C", 5), ("y_up", 1, 0), ("on_dn", 4),
    ("y_dn", 1, 0), ("y_up", 1, 1), ("y_dn", 1, 1), ("on_up", 4), ("update", 3), ("end", 0, 0), ("y_up", 1, 2),
    ("y_dn", 1, 2), ("end", 0, 1), ("end", 0, 2), ("y_up", 1, 3), ("y_dn", 1, 3), ("on_up", 5), ("last_own", 0, 3),
    ("on_dn", 5), ("last", 1, 0), ("last", 1, 1), ("last", 1, 2), ("last", 1, 3), ("update", 4), ("end", 1, 0),
    ("update", 5), ("end", 1, 1), ("end", 1, 2), ("end", 1, 3),
)
DRAINS = {("turn", 3): ("A", 3), ("end", 1, 0): ("B", 5)}
PARTS = 2


def kernel(
    tok_in, noise_in, cot_in, mean_in, hess_in, mom_in,
    mean_out, hess_out, mom_out, din_out,
    tok, tokt, n_own, n_par, ms, wt, cot, mean_v, hess_v, mom_v,
    pre_own, p_send, p_recv, dp, dpt,
    up_send, up_recv, dn_send, dn_recv, up2_send, up2_recv, dn2_send, dn2_recv, g_keep, g_own,
    c_send, c_recv, c_own, yu_send, yu_recv, yd_send, yd_recv, yu2_send, yu2_recv, yd2_send, yd2_recv,
    x_send, x_recv, f_send, f_recv, f_own, o_buf,
    ssem, rsem, lsem,
):
    rep, tp = lax.axis_index("rep"), lax.axis_index("tp")
    z, h = rep // 2, rep % 2
    y, l, c = tp // 4, (tp // 2) % 2, tp % 2

    def at(z=z, h=h, y=y, l=l, c=c):
        return (z * 2 + h, (y * 2 + l) * 2 + c)

    def zz(k):
        return lax.rem(z + k, NZ)

    def yy(k):
        return lax.rem(y + k, NY)

    partner, other_core, other_l = at(h=1 - h), at(c=1 - c), at(l=1 - l)
    z_up, z_dn, y_up, y_dn = at(z=zz(1)), at(z=zz(3)), at(y=yy(1)), at(y=yy(3))
    count = [2]
    sent = []

    def remote(src, dst, device, slot, rslot):
        return pltpu.make_async_remote_copy(
            src_ref=src, dst_ref=dst, send_sem=ssem.at[slot], recv_sem=rsem.at[rslot],
            device_id=device, device_id_type=MESH,
        )

    def send(src, dst, device, start=True):
        slot = count[0]
        count[0] += 1
        copy = remote(src, dst, device, slot, slot)
        if start:
            copy.start()
        sent.append(copy)
        return copy

    peers = [other_l, partner, at(h=1 - h, l=1 - l), other_core, z_up, z_dn, y_up, y_dn]
    barrier = pltpu.get_barrier_semaphore()
    for peer in peers:
        pl.semaphore_signal(barrier, inc=1, device_id=peer, device_id_type=MESH)

    loads = []

    def load(src, dst):
        copy = pltpu.make_async_copy(src, dst, lsem.at[len(loads)])
        copy.start()
        loads.append(copy)
        return copy

    load_mean, load_hess = load(mean_in, mean_v), load(hess_in, hess_v)
    pl.semaphore_wait(barrier, len(peers))

    def tok_slot(s, at_y):
        return tok.at[s, :, pl.ds(pl.multiple_of(at_y * 512 + c * 256, 256), 256)]

    t_near = remote(tok_in, tok_slot(h, y), at(h=l, l=1 - l), 0, h)
    t_near.start()
    t_far = remote(tok_in, tok_slot(h, y), partner, 1, h)
    t_self = pltpu.make_async_copy(tok_in, tok_slot(h, y), rsem.at[h])
    stays = h == l

    @pl.when(stays)
    def _():
        t_self.start()

    @pl.when(jnp.logical_not(stays))
    def _():
        t_far.start()

    n_copies = []

    def send_noise(upto, start=True):
        for n in range(len(n_copies), min(upto, NZ * len(CHUNKS))):
            (first, rows), b = CHUNKS[n // NZ], n % NZ
            n_copies.append(
                send(
                    noise_in.at[pl.ds(first, rows), pl.ds(pl.multiple_of((2 * b + 1 - h) * BLOCK, BLOCK), BLOCK)],
                    n_par.at[pl.ds(first, rows), pl.ds(b * BLOCK, BLOCK)],
                    partner,
                    start,
                )
            )

    send_noise(ORDER[0][1])
    load_own = [
        load(
            noise_in.at[:, pl.ds(pl.multiple_of((2 * b + h) * BLOCK, BLOCK), BLOCK)],
            n_own.at[:, pl.ds(b * BLOCK, BLOCK)],
        )
        for b in range(NZ)
    ]
    load_cot, load_mom = load(cot_in, cot), load(mom_in, mom_v)

    def z_block(k):
        return pl.ds(pl.multiple_of(zz(k) * BLOCK, BLOCK), BLOCK)

    own_z = z_block(0)
    s_up, s_dn, s_up2, s_dn2 = {}, {}, {}, {}

    def state(k):
        first, rows = CHUNKS[k]

        @pl.loop(0, rows // 16)
        def _(i):
            r = pl.ds(pl.multiple_of(first + i * 16, 16), 16)
            ms[0, r, own_z] = mean_v[r, :].astype(BF)
            ms[1, r, own_z] = lax.rsqrt(4.0 * (hess_v[r, :] + 0.001)).astype(BF)

        part = ms.at[:, pl.ds(first, rows), own_z]
        s_up[k], s_dn[k] = send(part, part, z_up), send(part, part, z_dn)

    def state_up(k):
        s_up[k].wait_recv()
        part = ms.at[0, pl.ds(*CHUNKS[k]), z_block(3)]
        s_up2[k] = send(part, part, z_up)

    def state_dn(k):
        s_dn[k].wait_recv()
        part = ms.at[1, pl.ds(*CHUNKS[k]), z_block(1)]
        s_dn2[k] = send(part, part, z_dn)

    load_mean.wait()
    load_hess.wait()

    t_up, t_dn, core = {}, {}, []

    def token(k):
        s = 1 - h if k else h
        slot = tok_slot(s, y)
        pltpu.make_async_copy(slot, slot, rsem.at[s]).wait()
        t_up[k] = send(slot, slot, y_up)
        t_dn[k] = send(slot, slot, y_dn)
        core.append(send(slot, slot, other_core))

    def token_up(k):
        t_up[k].wait_recv()
        slot = tok_slot(1 - h if k == 1 else h, yy(2 if k == 2 else 3))
        core.append(send(slot, slot, other_core))
        if k == 0:
            t_up[2] = send(slot, slot, y_up)

    def token_dn(k):
        t_dn[k].wait_recv()
        slot = tok_slot(h if k == 0 else 1 - h, yy(2 if k == 2 else 1))
        core.append(send(slot, slot, other_core))
        if k == 1:
            t_dn[2] = send(slot, slot, y_dn)

    def tokens(_):
        for copy in core:
            copy.wait_recv()

        @pl.loop(0, 2 * WIDE // 256)
        def _(i):
            s, b = i // 8, i % 8
            f = pl.ds(pl.multiple_of(b * 256, 256), 256)
            tokt[s, f, :] = tok[s, :, f].T

        load_cot.wait()
        for copy in load_own:
            copy.wait()

    p_copies, d_copies = {}, {}

    def weights_and_pre(k):
        first, rows = CHUNKS[k]
        span = pl.ds(first, rows)
        for copy in (s_up2[k], s_dn2[k], *n_copies[NZ * k : NZ * k + NZ]):
            copy.wait_recv()

        @pl.loop(0, rows // 16)
        def _(i):
            r = pl.ds(pl.multiple_of(first + i * 16, 16), 16)
            for b in range(NZ):
                f = pl.ds(b * BLOCK, BLOCK)
                m, g = ms[0, r, f].astype(F32), ms[1, r, f].astype(F32)
                wt[0, r, f] = (m + g * n_own[r, f].astype(F32)).astype(BF)
                wt[1, r, f] = (m + g * n_par[r, f].astype(F32)).astype(BF)

        for half in range(2):
            t = pl.ds(half * HALF, HALF)
            p_send[span, t] = jnp.dot(wt[1, span, :], tokt[1 - h, :, t], preferred_element_type=F32).astype(BF)
        p_copies[k] = send(p_send.at[span], p_recv.at[span], partner)
        for half in range(2):
            t = pl.ds(half * HALF, HALF)
            pre_own[span, t] = jnp.dot(wt[0, span, :], tokt[h, :, t], preferred_element_type=F32)

    def turn(s, k):
        span = pl.ds(*CHUNKS[k])
        for t in range(16):
            if t % 4 == 0:
                turned = dp[s, span, t * 32 : t * 32 + 128].T
            dpt[s, t % 2, pl.ds(t // 2 * 32, 32), span] = turned[t % 4 * 32 : t % 4 * 32 + 32, :]

    def dpre(k):
        first, rows = CHUNKS[k]
        span = pl.ds(first, rows)
        p_copies[k].wait_recv()

        @pl.loop(0, rows // 16)
        def _(i):
            r = pl.ds(pl.multiple_of(first + i * 16, 16), 16)
            pre = pre_own[r, :] + p_recv[r, :].astype(F32)
            sig = 1.0 / (1.0 + jnp.exp(-pre))
            dp[0, r, :] = (cot[r, :].astype(F32) * sig * (1.0 + pre * (1.0 - sig))).astype(BF)

        d_copies[k] = send(dp.at[0, span], dp.at[1, span], partner)
        turn(0, k)

    g_up, g_dn, g_up2, g_dn2 = {}, {}, {}, {}

    came = set()

    def dpre_here(k):
        if k not in came:
            d_copies[k].wait_recv()
            came.add(k)

    def turn_other(k):
        dpre_here(k)
        turn(1, k)

    def grads(k):
        dpre_here(k)
        span = pl.ds(*CHUNKS[k])
        for step in (2, 1, 3, 0):
            for half in range(2):
                t = pl.ds(half * HALF, HALF)
                f = pl.ds(pl.multiple_of(zz(step) * BLOCK + half * HALF, HALF), HALF)
                one = jnp.dot(dp[0, span, :], tok[h, :, f], preferred_element_type=F32)
                two = jnp.dot(dp[1, span, :], tok[1 - h, :, f], preferred_element_type=F32)
                grad, hest = one + two, one * n_own[span, f].astype(F32) + two * n_par[span, f].astype(F32)
                if step == 2:
                    up_send[0, span, t] = grad.astype(BF)
                    dn_send[0, span, t] = hest.astype(BF)
                elif step == 1:
                    g_keep[0, span, t] = grad
                    up_send[1, span, t] = hest.astype(BF)
                elif step == 3:
                    dn_send[1, span, t] = grad.astype(BF)
                    g_keep[1, span, t] = hest
                else:
                    g_own[0, span, t] = grad
                    g_own[1, span, t] = hest
            if step == 1:
                g_up[k] = send(up_send.at[:, span], up_recv.at[:, span], z_up)
            elif step == 3:
                g_dn[k] = send(dn_send.at[:, span], dn_recv.at[:, span], z_dn)

    def on_up(k):
        span = pl.ds(*CHUNKS[k])
        g_up[k].wait_recv()
        up2_send[span, :] = (g_keep[0, span, :] + up_recv[0, span, :].astype(F32)).astype(BF)
        g_up2[k] = send(up2_send.at[span], up2_recv.at[span], z_up)

    def on_dn(k):
        span = pl.ds(*CHUNKS[k])
        g_dn[k].wait_recv()
        dn2_send[span, :] = (g_keep[1, span, :] + dn_recv[0, span, :].astype(F32)).astype(BF)
        g_dn2[k] = send(dn2_send.at[span], dn2_recv.at[span], z_dn)

    stores = []

    def store(src, dst):
        copy = pltpu.make_async_copy(src, dst, lsem.at[len(loads) + len(stores)])
        copy.start()
        stores.append(copy)

    def update(k):
        first, rows = CHUNKS[k]
        if k == 0:
            load_mom.wait()
        span = pl.ds(first, rows)
        g_up2[k].wait_recv()
        g_dn2[k].wait_recv()

        @pl.loop(0, rows // 16)
        def _(i):
            r = pl.ds(pl.multiple_of(first + i * 16, 16), 16)
            mean, hess = mean_v[r, :], hess_v[r, :]
            grad_mean = (g_own[0, r, :] + dn_recv[1, r, :].astype(F32) + up2_recv[r, :].astype(F32)) / 8.0
            hest = (g_own[1, r, :] + up_recv[1, r, :].astype(F32) + dn2_recv[r, :].astype(F32)) / 8.0
            hess_mean = hest / ms[1, r, own_z].astype(F32)
            new_momentum = 0.9 * mom_v[r, :] + 0.1 * grad_mean
            diff = hess - hess_mean
            new_hess = hess + 0.2 * (hess_mean - hess) + 0.5 * 0.04 * diff * diff / (hess + 0.001)
            mom_v[r, :] = new_momentum
            hess_v[r, :] = new_hess
            mean_v[r, :] = mean - 0.5 * (new_momentum + 0.001 * mean) / (new_hess + 0.001)

        store(mean_v.at[span], mean_out.at[span])
        store(hess_v.at[span], hess_out.at[span])
        store(mom_v.at[span], mom_out.at[span])

    c_copies, y_up1, y_dn1, y_up2, y_dn2, f_copies = {}, {}, {}, {}, {}, {}

    def din_product(s, p, keep):
        f = pl.ds(p * PW, PW)
        for q in range(PW // HALF):
            g = pl.ds(p * PW + q * HALF, HALF)
            part = jnp.dot(dpt[s, c if keep else 1 - c], wt[s, :, g], preferred_element_type=F32)
            if keep:
                c_own[s, :, g] = part
            else:
                c_send[s, :, g] = part.astype(BF)
        if not keep:
            c_copies[s, p] = send(c_send.at[s, :, f], c_recv.at[s, :, f], other_core)

    x_copies = {}

    def din_x_first(s, p):
        c_copies[s, p].wait_recv()
        at_x = X_FIRST.index((s, p))
        f = pl.ds(p * PW, PW)
        for k in range(NY):
            rows = pl.ds(pl.multiple_of(k * 64 + (1 - l) * 32, 32), 32)
            x_send[at_x, pl.ds(k * 32, 32), :] = (c_own[s, rows, f] + c_recv[s, rows, f].astype(F32)).astype(BF)
        x_copies[s, p] = send(x_send.at[at_x], x_recv.at[at_x], other_l)

    def depth(s, p):
        return 32 if (s, p) in X_FIRST else 64

    def din_sum(s, p, k, second):
        g = pl.ds(p * PW + second * PH, PH)
        if (s, p) in X_FIRST:
            rows = pl.ds(pl.multiple_of(yy(k) * 64 + l * 32, 32), 32)
            there = pl.ds(pl.multiple_of(yy(k) * 32, 32), 32)
            return c_own[s, rows, g] + (
                c_recv[s, rows, g].astype(F32) + x_recv[X_FIRST.index((s, p)), there, pl.ds(second * PH, PH)].astype(F32)
            )
        rows = pl.ds(pl.multiple_of(yy(k) * 64, 64), 64)
        return c_own[s, rows, g] + c_recv[s, rows, g].astype(F32)

    def din_y(s, p):
        (x_copies if (s, p) in X_FIRST else c_copies)[s, p].wait_recv()
        d = pl.ds(0, depth(s, p))
        yu_send[s, p, 0, d] = din_sum(s, p, 2, 0).astype(BF)
        yu_send[s, p, 1, d] = din_sum(s, p, 1, 1).astype(BF)
        y_up1[s, p] = send(yu_send.at[s, p, :, d], yu_recv.at[s, p, :, d], y_up)
        yd_send[s, p, 0, d] = din_sum(s, p, 2, 1).astype(BF)
        yd_send[s, p, 1, d] = din_sum(s, p, 3, 0).astype(BF)
        y_dn1[s, p] = send(yd_send.at[s, p, :, d], yd_recv.at[s, p, :, d], y_dn)

    def din_y_up(s, p):
        d = pl.ds(0, depth(s, p))
        y_up1[s, p].wait_recv()
        yu2_send[s, p, d] = (din_sum(s, p, 1, 0) + yu_recv[s, p, 0, d].astype(F32)).astype(BF)
        y_up2[s, p] = send(yu2_send.at[s, p, d], yu2_recv.at[s, p, d], y_up)

    def din_y_dn(s, p):
        d = pl.ds(0, depth(s, p))
        y_dn1[s, p].wait_recv()
        yd2_send[s, p, d] = (din_sum(s, p, 3, 1) + yd_recv[s, p, 0, d].astype(F32)).astype(BF)
        y_dn2[s, p] = send(yd2_send.at[s, p, d], yd2_recv.at[s, p, d], y_dn)

    def din_last_own(s, p):
        y_up2[s, p].wait_recv()
        y_dn2[s, p].wait_recv()
        d = pl.ds(0, depth(s, p))
        for second in range(2):
            part = din_sum(s, p, 0, second)
            if second:
                part = part + yu_recv[s, p, 1, d].astype(F32) + yd2_recv[s, p, d].astype(F32)
            else:
                part = part + yd_recv[s, p, 1, d].astype(F32) + yu2_recv[s, p, d].astype(F32)
            first = p * PW + second * PH
            there = (2 * (first // BLOCK) + h) * BLOCK + first % BLOCK
            o_buf[:, pl.ds(pl.multiple_of(there, PH), PH)] = part.astype(BF)

    def din_last(s, p):
        y_up2[s, p].wait_recv()
        y_dn2[s, p].wait_recv()
        f = pl.ds(p * PW, PW)
        f_copies[s, p] = []
        for near in (False, True):
            which = l if near else 1 - l
            mine = pl.ds(pl.multiple_of(y * 64 + which * 32, 32), 32)
            rows = pl.ds(pl.multiple_of(which * 32, 32), 32)
            for second in range(2):
                g = pl.ds(p * PW + second * PH, PH)
                part = c_own[s, mine, g] + c_recv[s, mine, g].astype(F32)
                if second:
                    part = part + yu_recv[s, p, 1, rows, :].astype(F32) + yd2_recv[s, p, rows, :].astype(F32)
                else:
                    part = part + yd_recv[s, p, 1, rows, :].astype(F32) + yu2_recv[s, p, rows, :].astype(F32)
                if near and not s:
                    f_own[:, g] = part
                else:
                    f_send[s + near, :, g] = part.astype(BF)
            if s or not near:
                there = partner if near else at(h=1 - h, l=1 - l) if s else other_l
                f_copies[s, p].append(send(f_send.at[s + near, :, f], f_recv.at[s + near, :, f], there))

    def din_end(s, p):
        for copy in f_copies[s, p]:
            copy.wait_recv()
        for b in range(p * PW // BLOCK, (p + 1) * PW // BLOCK):
            f = pl.ds(b * BLOCK, BLOCK)
            there = pl.ds(pl.multiple_of((2 * b + (1 - h if s else h)) * BLOCK, BLOCK), BLOCK)
            if s:
                part = f_recv[1, :, f].astype(F32) + f_recv[2, :, f].astype(F32)
            else:
                part = f_own[:, f] + f_recv[0, :, f].astype(F32)
            o_buf[:, there] = part.astype(BF)

    steps = {
        "noise": send_noise, "state": state, "state_up": state_up, "state_dn": state_dn,
        "token": token, "token_up": token_up, "token_dn": token_dn, "tokens": tokens,
        "A": weights_and_pre, "B": dpre, "turn": turn_other, "C": grads,
        "on_up": on_up, "on_dn": on_dn, "update": update,
        "prod_send": lambda s, p: din_product(s, p, False), "prod_own": lambda s, p: din_product(s, p, True),
        "x_first": din_x_first, "y": din_y, "y_up": din_y_up, "y_dn": din_y_dn,
        "last": din_last, "last_own": din_last_own, "end": din_end,
    }
    marks, drained = {}, 0
    for step in ORDER:
        marks[step] = len(sent)
        if step in DRAINS:
            upto = marks[DRAINS[step]]
            for copy in sent[drained:upto]:
                copy.wait_send()
            drained = upto
        name, *where = step
        steps[name](*where)
    store(o_buf, din_out)
    for copy in stores:
        copy.wait()
    t_near.wait_send()

    @pl.when(jnp.logical_not(stays))
    def _():
        t_far.wait_send()

    for copy in sent[drained:]:
        copy.wait_send()


def settle(*refs):
    n = len(refs) // 2
    for src, dst in zip(refs[:n], refs[n:]):
        dst[...] = src[...]


def shards(tokens, noise, cotangent, mean, hess, momentum):
    vm = pltpu.VMEM
    units = (UNITS, BLOCK)
    piece = (2, PIECES, 64, PH)
    scratch = [
        vm((2, BLOCK, WIDE), BF),
        vm((2, WIDE, BLOCK), BF),
        vm((UNITS, WIDE), BF),
        vm((UNITS, WIDE), BF),
        vm((2, UNITS, WIDE), BF),
        vm((2, UNITS, WIDE), BF),
        vm(units, BF),
        vm(units, F32),
        vm(units, F32),
        vm(units, F32),
        vm(units, F32),
        vm(units, BF),
        vm(units, BF),
        vm((2,) + units, BF),
        vm((2, 2, HALF, UNITS), BF),
        *[vm((2,) + units, BF)] * 4,
        *[vm(units, BF)] * 4,
        vm((2,) + units, F32),
        vm((2,) + units, F32),
        vm((2, HALF, WIDE), BF),
        vm((2, HALF, WIDE), BF),
        vm((2, HALF, WIDE), F32),
        *[vm((2, PIECES, 2, 64, PH), BF)] * 4,
        *[vm(piece, BF)] * 4,
        vm((len(X_FIRST), 128, PW), BF),
        vm((len(X_FIRST), 128, PW), BF),
        vm((3, 32, WIDE), BF),
        vm((3, 32, WIDE), BF),
        vm((32, WIDE), F32),
        vm((32, 2 * WIDE), BF),
        pltpu.SemaphoreType.DMA((N_SEM,)),
        pltpu.SemaphoreType.DMA((N_SEM,)),
        pltpu.SemaphoreType.DMA((32,)),
    ]
    anywhere = pl.BlockSpec(memory_space=pl.ANY)
    outs = [jax.ShapeDtypeStruct(units, F32)] * 3 + [jax.ShapeDtypeStruct((32, 2 * WIDE), BF)]
    results = pl.pallas_call(
        kernel,
        out_shape=outs,
        in_specs=[anywhere] * 6,
        out_specs=[anywhere] * 4,
        scratch_shapes=scratch,
        compiler_params=pltpu.CompilerParams(
            collective_id=1, has_side_effects=True, vmem_limit_bytes=63 << 20
        ),
        cost_estimate=pl.CostEstimate(flops=9 * 10**9, bytes_accessed=20 * 2**20, transcendentals=10**6),
    )(tokens, noise[0].T, cotangent.T, mean.T, hess.T, momentum.T)
    blocks = [pl.BlockSpec((o.shape[0] // PARTS, o.shape[1]), lambda i: (i, 0)) for o in outs]
    new_mean, new_hess, new_momentum, input_grad = pl.pallas_call(
        settle,
        grid=(PARTS,),
        out_shape=outs,
        in_specs=blocks,
        out_specs=blocks,
        compiler_params=pltpu.CompilerParams(vmem_limit_bytes=63 << 20),
        cost_estimate=pl.CostEstimate(flops=0, bytes_accessed=9 * 2**20, transcendentals=0),
    )(*results)
    return (new_mean.T, new_hess.T, new_momentum.T, input_grad)


def solution(mesh):
    in_specs = (
        P("rep", "tp"),
        P("rep", None, "tp"),
        P("rep", "tp"),
        P("rep", "tp"),
        P("rep", "tp"),
        P("rep", "tp"),
    )
    out_specs = (P("rep", "tp"), P("rep", "tp"), P("rep", "tp"), P(("rep", "tp"), None))
    return jax.shard_map(shards, mesh=mesh, in_specs=in_specs, out_specs=out_specs, check_vma=False)
```
